32 devices in a mesh: ctx: 8 (over y, x, core), tp: 4 (over z).
Axes of the slice: x: 2, y: 2, z: 4, core: 2. Of those that a mesh axis runs over, the one named last changes fastest.
Arguments:
- queries: bfloat16 [2048, 8192], P('ctx', 'tp'), may hold values from -100 to 100
- key_rows: bfloat16 [2048, 1024], P('ctx'), may hold values from -5 to 5
- value_rows: bfloat16 [2048, 1024], P('ctx'), may hold values from -6 to 6
- documents: int32 [2048], P('ctx'), may hold values from 0 to 3, never falling along the last dimension, each value on 1 to 1536 neighbouring positions
- out_weight: bfloat16 [8192, 8192], P('tp', 'ctx'), may hold values from -0.75 to 0.75
Outputs:
- attention_out: bfloat16 [2048, 8192], P(('ctx', 'tp'))
The draws below stay inside these ranges and needn't reach their ends.
Inputs may be any that keep to these rules, and one draw needn't show every extreme that they name: `documents`: document numbers never fall along the window; each document holds 1 to 1536 tokens and one holds exactly 1536.
All inputs are finite; a program needn't handle non-finite values.
Results may differ from the reference program's by a relative error of at most 0.015.
Values may be sent and summed in bfloat16 or wider, within the bound.
A program may use at most 128 MiB of HBM per device.

```python
import math
import jax
import jax.numpy as jnp
import numpy as np
from jax import lax

D = 8192
HEADS = 64
KV_HEADS = 8
HD = 128
DOCS = 4
SEQ = 2048
MOST = 1536
N_TP = 4


def draw_together(key):
    key_base = jnp.clip(jax.random.normal(jax.random.fold_in(key, 101), (SEQ, KV_HEADS, HD), jnp.float32), -4.5, 4.5)
    query_base = jnp.clip(jax.random.normal(jax.random.fold_in(key, 102), (SEQ, HEADS, HD), jnp.float32), -5.0, 5.0)
    return (query_base.reshape(SEQ, HEADS * HD), key_base.reshape(SEQ, KV_HEADS * HD))


def draw_queries(key, part):
    return draw_together(key)[0].astype(jnp.bfloat16)


def draw_key_rows(key, part):
    return draw_together(key)[1].astype(jnp.bfloat16)


def steps_of(rng, extent, shards, least, largest):
    level = 1.0
    for axis_at, shards_of in shards:
        heights = jax.random.uniform(jax.random.fold_in(jax.random.fold_in(rng, 6), axis_at), (shards_of,), jnp.float32, least / len(shards), largest / len(shards))
        level = level * jnp.repeat(jnp.exp(heights), extent[axis_at] // shards_of).reshape((-1,) + (1,) * (len(extent) - 1 - axis_at))
    return level


def profile(count, total, most, skew):
    weights = [(1 << 20) // math.isqrt(grade ** skew) + 1 for grade in range(2, count + 1)]
    surplus, counts = total - most - (count - 1), [1] * (count - 1)
    while surplus > 0:
        movable = [i for i in range(count - 1) if counts[i] < most]
        pool, budget = sum([weights[i] for i in movable]), surplus
        for i in movable:
            addition = min(most - counts[i], max(1, budget * weights[i] // pool), surplus)
            counts[i] = counts[i] + addition
            surplus = surplus - addition
    return np.array([most] + counts)


def ragged_sizes(key, number_of, total, bound, lean):
    if number_of == 2:
        one = jax.random.randint(key, (), max(1, total - bound), min(bound, total - 1) + 1)
        return jnp.stack([one, total - one])
    tallies = jnp.asarray(profile(number_of, total, bound, lean), jnp.int32)
    pairs = (number_of - 1) // 2
    source_of, sink = tallies[1:1 + 2 * pairs:2], tallies[2:2 + 2 * pairs:2]
    room = jnp.minimum(source_of - 1, bound - sink)
    moved = jax.random.randint(jax.random.fold_in(key, 1), (pairs,), 0, 1 << 20) % (room + 1)
    tallies = tallies.at[1:1 + 2 * pairs:2].set(source_of - moved).at[2:2 + 2 * pairs:2].set(sink + moved)
    return tallies[jax.random.permutation(jax.random.fold_in(key, 2), number_of)]


def gaussian(rng, extent, deviation, reach, split=(), held_as=jnp.bfloat16):
    factor_of = steps_of(rng, extent, split, -0.22, 0.18) if split else 1.0
    values = jax.random.normal(rng, extent, jnp.float32) * deviation * factor_of
    return jnp.minimum(jnp.maximum(values, -reach), reach).astype(held_as)


def setup_inputs(seed: int = 0) -> dict:
    key_list = jax.random.split(jax.random.key(seed), 6)
    return {
        "queries": draw_queries(jax.random.fold_in(key_list[5], 71), 0),
        "key_rows": draw_key_rows(jax.random.fold_in(key_list[5], 71), 0),
        "value_rows": gaussian(key_list[2], (SEQ, KV_HEADS * HD), 1.0, 6.0, ((0, 8),)),
        "documents": jnp.searchsorted(jnp.cumsum(ragged_sizes(key_list[3], DOCS, SEQ, MOST, 0)), jnp.arange(SEQ), side="right").astype(jnp.int32),
        "out_weight": gaussian(key_list[4], (HEADS * HD, D), (HD // 2) ** -0.5, 0.75, ((0, 4), (1, 8))),
    }


def head_output(queries, key_rows, value_rows, documents, head_index):
    group_size = HEADS // KV_HEADS
    query_cols = lax.dynamic_slice_in_dim(queries, (head_index * HD).astype(jnp.int32), HD, 1)
    kv_start = (head_index // group_size * HD).astype(jnp.int32)
    key_cols = lax.dynamic_slice_in_dim(key_rows, kv_start, HD, 1)
    value_cols = lax.dynamic_slice_in_dim(value_rows, kv_start, HD, 1)
    scores = jnp.dot(query_cols, key_cols.T, preferred_element_type=jnp.float32) * (1.0 / math.sqrt(HD))
    position = jnp.arange(SEQ, dtype=jnp.int32)
    allowed = (position[None, :] <= position[:, None]) & (documents[None, :] == documents[:, None])
    row_max = lax.optimization_barrier(jnp.max(jnp.where(allowed, scores, -1e+30), axis=1, keepdims=True))
    weights = jnp.where(allowed, jnp.exp(scores - row_max), 0.0)
    denominator = lax.optimization_barrier(jnp.sum(weights, axis=1, keepdims=True))
    weighted = jnp.dot(weights.astype(jnp.bfloat16), value_cols, preferred_element_type=jnp.float32)
    return (weighted / denominator).astype(jnp.bfloat16)

def reference(queries, key_rows, value_rows, documents, out_weight):
    heads_out = lax.map(lambda head_index: head_output(queries, key_rows, value_rows, documents, head_index), jnp.arange(HEADS, dtype=jnp.int32))
    attended = jnp.transpose(heads_out, (1, 0, 2)).reshape(SEQ, HEADS * HD)
    block_width = HEADS * HD // N_TP

    def accumulate(group_index, running):
        begin = (group_index * block_width).astype(jnp.int32)
        columns = lax.dynamic_slice_in_dim(attended, begin, block_width, 1)
        weight_rows = lax.dynamic_slice_in_dim(out_weight, begin, block_width, 0)
        partial_sum = jnp.dot(columns, weight_rows, preferred_element_type=jnp.float32)
        rounded = lax.optimization_barrier(partial_sum.astype(jnp.bfloat16))
        return running + rounded.astype(jnp.float32)
    summed = lax.fori_loop(0, N_TP, accumulate, jnp.zeros((SEQ, D), jnp.float32))
    return summed.astype(jnp.bfloat16)
```

```python
import functools
import math

import jax
import jax.numpy as jnp
from jax import lax
from jax.experimental import pallas as pl
from jax.experimental.pallas import tpu as pltpu
from jax.sharding import PartitionSpec as P

HEADS = 64
KV_HEADS = 8
HD = 128
MESH = pl.DeviceIdType.MESH
F32 = jnp.float32
BF16 = jnp.bfloat16
SCALE2 = math.log2(math.e) / math.sqrt(HD)
UNITS = 4


def fused_kernel(
    q_ref, k_ref, v_ref, dcol_ref, drow_ref, w_hbm, out_ref,
    w_ref, kv, docs, att, part, zin, fin,
    w_sem, kv_send, kv_recv, doc_send, doc_recv,
    att_send, att_recv, z_send, z_recv, x_send, x_recv,
):
    c = lax.axis_index("ctx")
    z = lax.axis_index("tp")
    ctx = kv.shape[0]
    tokens = q_ref.shape[0]
    rows = att.shape[2]
    kv_here = kv.shape[2] // (2 * HD)
    per_kv = q_ref.shape[1] // HD // kv_here
    unit = part.shape[3]
    width = UNITS * unit

    y, x, core = c // 4, (c // 2) % 2, c % 2

    def at(yy, xx, cc):
        return yy * 4 + xx * 2 + cc

    sib, xn, yn = at(y, x, 1 - core), at(y, 1 - x, core), at(1 - y, x, core)
    dg = at(1 - y, 1 - x, core)
    sib_xn, sib_yn = at(y, 1 - x, 1 - core), at(1 - y, x, 1 - core)
    sib_dg = at(1 - y, 1 - x, 1 - core)

    far = z // 2
    out = 1 - 2 * far
    mid = z * (1 - far) + (3 - z) * far
    ahead, behind = z + out, z - out

    def chunk(p):
        mirrored = (1 - mid) * (3 - p) + mid * (3, 0, 2, 1)[p]
        return mirrored * (1 - far) + (3 - mirrored) * far

    def remote(src, dst, ss, rs, device):
        return pltpu.make_async_remote_copy(
            src_ref=src, dst_ref=dst, send_sem=ss, recv_sem=rs,
            device_id=device, device_id_type=MESH,
        )

    w_copy = pltpu.make_async_copy(w_hbm, w_ref, w_sem)
    w_copy.start()

    barrier = pltpu.get_barrier_semaphore()
    for step in range(1, ctx):
        pl.semaphore_signal(
            barrier, inc=1, device_id=(lax.rem(c + step, ctx), z), device_id_type=MESH
        )
    pl.semaphore_signal(barrier, inc=1, device_id=(c, ahead), device_id_type=MESH)

    @pl.when(mid == 1)
    def _():
        pl.semaphore_signal(barrier, inc=1, device_id=(c, behind), device_id_type=MESH)

    first = pl.multiple_of(z * kv_here * HD, kv_here * HD)
    kv[c, :, : kv_here * HD] = k_ref[:, pl.ds(first, kv_here * HD)]
    kv[c, :, kv_here * HD :] = v_ref[:, pl.ds(first, kv_here * HD)]
    docs[c] = jnp.broadcast_to(drow_ref[...], docs.shape[1:])
    pl.semaphore_wait(barrier, ctx + mid)

    def moves(buf, ss, rs):
        half = buf.shape[1] // 2
        lower, upper = pl.ds(0, half), pl.ds(half, half)
        own = [
            remote(buf.at[c], buf.at[c], ss.at[0], rs.at[0], (sib, z)),
            remote(buf.at[c], buf.at[c], ss.at[1], rs.at[1], (xn, z)),
            remote(buf.at[c], buf.at[c], ss.at[2], rs.at[2], (yn, z)),
        ]
        fwd = [
            remote(buf.at[xn, lower], buf.at[xn, lower], ss.at[3], rs.at[3], (yn, z)),
            remote(buf.at[yn, upper], buf.at[yn, upper], ss.at[4], rs.at[4], (xn, z)),
            remote(buf.at[xn], buf.at[xn], ss.at[5], rs.at[5], (sib, z)),
            remote(buf.at[yn], buf.at[yn], ss.at[6], rs.at[6], (sib, z)),
            remote(buf.at[dg, lower], buf.at[dg, lower], ss.at[7], rs.at[7], (sib, z)),
            remote(buf.at[dg, upper], buf.at[dg, upper], ss.at[8], rs.at[8], (sib, z)),
        ]

        def got(n, view):
            remote(view, view, ss.at[n], rs.at[n], (sib, z)).wait_recv()

        def start_own():
            for copy in own:
                copy.start()

        def forward_near():
            got(1, buf.at[xn])
            fwd[0].start()
            fwd[2].start()
            got(2, buf.at[yn])
            fwd[1].start()
            fwd[3].start()

        def forward_diagonal():
            got(3, buf.at[dg, lower])
            fwd[4].start()
            got(4, buf.at[dg, upper])
            fwd[5].start()

        def all_in():
            got(0, buf.at[sib])
            got(5, buf.at[sib_xn])
            got(6, buf.at[sib_yn])
            got(7, buf.at[sib_dg, lower])
            got(8, buf.at[sib_dg, upper])

        def all_sent():
            for copy in own + fwd:
                copy.wait_send()

        return start_own, forward_near, forward_diagonal, all_in, all_sent

    kv_moves = moves(kv, kv_send, kv_recv)
    kv_moves[0]()
    doc_copies = []
    for step in range(1, ctx):
        peer = lax.rem(c + step, ctx)
        doc_copies.append(
            remote(docs.at[c], docs.at[c], doc_send.at[step], doc_recv.at[step], (peer, z))
        )
        doc_copies[-1].start()
    kv_moves[1]()
    kv_moves[2]()
    for step in range(1, ctx):
        source = lax.rem(c + ctx - step, ctx)
        remote(
            docs.at[source], docs.at[source], doc_send.at[step], doc_recv.at[step], (source, z)
        ).wait_recv()
    kv_moves[3]()

    pair = 2
    keys = pair * tokens
    blocks = c // pair + 1

    def attend(p):
        t = chunk(p)
        begin = pl.multiple_of(t * rows, rows)
        q_pos = c * tokens + t * rows + lax.broadcasted_iota(jnp.int32, (rows, keys), 0)
        q_doc = dcol_ref[pl.ds(begin, rows), :]
        for g in range(kv_here):
            q = jnp.concatenate(
                [
                    q_ref[pl.ds(begin, rows), (g * per_kv + h) * HD : (g * per_kv + h + 1) * HD]
                    for h in range(per_kv)
                ],
                axis=0,
            )

            def body(b, carry):
                old_max, acc = carry
                k = kv[pl.ds(pair * b, pair), :, g * HD : (g + 1) * HD].reshape(keys, HD)
                v = kv[
                    pl.ds(pair * b, pair), :, (kv_here + g) * HD : (kv_here + g + 1) * HD
                ].reshape(keys, HD)
                k_doc = jnp.concatenate(
                    [docs[pair * b + n][0:1, :] for n in range(pair)], axis=1
                )
                k_pos = b * keys + lax.broadcasted_iota(jnp.int32, (rows, keys), 1)
                bias = jnp.where((k_pos <= q_pos) & (k_doc == q_doc), 0.0, -1e30).astype(F32)
                s = lax.dot_general(
                    q, k, (((1,), (1,)), ((), ())), preferred_element_type=F32
                ) * SCALE2
                s = (s.reshape(per_kv, rows, keys) + bias[None]).reshape(per_kv * rows, keys)
                new_max = jnp.maximum(old_max, jnp.max(s, axis=1, keepdims=True))
                weights = jnp.exp2(s - new_max).astype(BF16)
                v_ones = jnp.concatenate([v, jnp.ones((keys, HD), BF16)], axis=1)
                acc = acc * jnp.exp2(old_max - new_max) + jnp.dot(
                    weights, v_ones, preferred_element_type=F32
                )
                return new_max, acc

            _, acc = lax.fori_loop(
                0,
                blocks,
                body,
                (
                    jnp.full((per_kv * rows, 1), -1e30, F32),
                    jnp.zeros((per_kv * rows, 2 * HD), F32),
                ),
            )
            o = (acc[:, :HD] / acc[:, HD:]).astype(BF16)
            for h in range(per_kv):
                att[p, c, :, (g * per_kv + h) * HD : (g * per_kv + h + 1) * HD] = o[
                    h * rows : (h + 1) * rows
                ]

    def project(p):
        def body(j, _):
            a = att[p].reshape(ctx * rows, att.shape[3])
            w = w_ref[:, pl.ds(pl.multiple_of(j * unit, unit), unit)]
            part[p, j] = jnp.dot(a, w, preferred_element_type=F32).astype(BF16)
            return 0

        lax.fori_loop(0, UNITS, body, 0)

    def end_hop(p, j):
        return remote(
            part.at[p, j], zin.at[(0, 2, 3)[p], j], z_send.at[p, j],
            z_recv.at[(0, 2, 3)[p], j], (c, ahead),
        )

    def mid_hop(p, j):
        return remote(
            part.at[p, j], zin.at[(1, 0, 4)[p], j], z_send.at[p, j],
            z_recv.at[(1, 0, 4)[p], j], (c, (ahead, behind, ahead)[p]),
        )

    def z_got(slot, j):
        remote(
            zin.at[slot, j], zin.at[slot, j], z_send.at[0, j], z_recv.at[slot, j], (c, ahead)
        ).wait_recv()

    def end_start(p):
        @pl.when(mid == 0)
        def _():
            for j in range(UNITS):
                end_hop(p, j).start()

    def pass_on(*units):
        @pl.when(mid == 1)
        def _():
            for p, j in units:
                z_got(p, j)
                part[p, j] = (part[p, j].astype(F32) + zin[p, j].astype(F32)).astype(BF16)
                mid_hop(p, j).start()

    w_copy.wait()
    steps = [
        moves(att.at[p], att_send.at[p], att_recv.at[p]) for p in range(4)
    ]
    attend(0)
    steps[0][0]()
    attend(1)
    steps[0][1]()
    steps[1][0]()
    steps[0][2]()
    steps[0][3]()
    project(0)
    end_start(0)
    attend(2)
    pass_on((0, 0))
    steps[1][1]()
    steps[2][0]()
    steps[1][2]()
    steps[1][3]()
    project(1)
    end_start(1)
    pass_on((0, 1), (1, 0))
    attend(3)
    steps[2][1]()
    steps[3][0]()
    steps[2][2]()
    steps[2][3]()
    project(2)
    end_start(2)
    pass_on((0, 2), (1, 1), (0, 3), (1, 2))
    steps[3][1]()
    steps[3][2]()
    steps[3][3]()
    project(3)
    pass_on((1, 3), (2, 0), (2, 1), (2, 2), (2, 3))

    x_copies = []
    for j in range(UNITS):
        @pl.when(mid == 0)
        def _():
            z_got(0, j)
            total = part[3, j].astype(F32) + zin[0, j].astype(F32)
            fin[j] = total.astype(BF16).reshape(fin.shape[1:])

        @pl.when(mid == 1)
        def _():
            z_got(4, j)
            z_got(3, j)
            total = part[3, j].astype(F32) + zin[3, j].astype(F32) + zin[4, j].astype(F32)
            fin[j] = total.astype(BF16).reshape(fin.shape[1:])

        columns = pl.ds(pl.multiple_of(c * width + j * unit, unit), unit)
        for step in range(1, ctx):
            peer = lax.rem(c + step, ctx)
            x_copies.append(
                remote(
                    fin.at[j, peer], out_ref.at[:, columns], x_send.at[step, j],
                    x_recv.at[step, j], (peer, z),
                )
            )
            x_copies[-1].start()
        out_ref[:, columns] = fin[j, c]

    for j in range(UNITS):
        for step in range(1, ctx):
            source = lax.rem(c + ctx - step, ctx)
            columns = pl.ds(pl.multiple_of(source * width + j * unit, unit), unit)
            remote(
                fin.at[j, source], out_ref.at[:, columns], x_send.at[step, j],
                x_recv.at[step, j], (source, z),
            ).wait_recv()

    kv_moves[4]()
    for copy in doc_copies + x_copies:
        copy.wait_send()
    for step in steps:
        step[4]()

    @pl.when(mid == 0)
    def _():
        for p in range(3):
            for j in range(UNITS):
                end_hop(p, j).wait_send()

    @pl.when(mid == 1)
    def _():
        for p in range(3):
            for j in range(UNITS):
                mid_hop(p, j).wait_send()


def fused(ctx, tp, queries, key_rows, value_rows, documents, out_weight):
    tokens, heads_width = queries.shape
    kv_here = heads_width // HD // (HEADS // KV_HEADS)
    rows = tokens // tp
    depth, width = out_weight.shape
    unit = width // UNITS
    vmem = pl.BlockSpec(memory_space=pltpu.VMEM)
    dma = pltpu.SemaphoreType.DMA
    return pl.pallas_call(
        fused_kernel,
        out_shape=jax.ShapeDtypeStruct((rows, width * ctx), BF16),
        in_specs=[vmem] * 5 + [pl.BlockSpec(memory_space=pl.ANY)],
        out_specs=vmem,
        scratch_shapes=[
            pltpu.VMEM((depth, width), BF16),
            pltpu.VMEM((ctx, tokens, 2 * kv_here * HD), BF16),
            pltpu.VMEM((ctx, 8, tokens), jnp.int32),
            pltpu.VMEM((tp, ctx, rows, heads_width), BF16),
            pltpu.VMEM((tp, UNITS, ctx * rows, unit), BF16),
            pltpu.VMEM((5, UNITS, ctx * rows, unit), BF16),
            pltpu.VMEM((UNITS, ctx, rows, unit), BF16),
            dma,
            dma((9,)),
            dma((9,)),
            dma((ctx,)),
            dma((ctx,)),
            dma((tp, 9)),
            dma((tp, 9)),
            dma((3, UNITS)),
            dma((5, UNITS)),
            dma((ctx, UNITS)),
            dma((ctx, UNITS)),
        ],
        compiler_params=pltpu.CompilerParams(
            collective_id=0, has_side_effects=True, vmem_limit_bytes=56 * 1024 * 1024
        ),
    )(
        queries, key_rows, value_rows, documents.reshape(tokens, 1),
        documents.reshape(1, tokens), out_weight,
    )


def general(ctx, tp, queries, key_rows, value_rows, documents, out_weight):
    tokens = queries.shape[0]
    heads_here = queries.shape[1] // HD
    group_size = HEADS // KV_HEADS
    kv_here = max(1, heads_here // group_size)
    per_kv = heads_here // kv_here
    kv_first = lax.axis_index("tp") * heads_here // group_size
    own_keys = lax.dynamic_slice_in_dim(key_rows, kv_first * HD, kv_here * HD, 1)
    own_values = lax.dynamic_slice_in_dim(value_rows, kv_first * HD, kv_here * HD, 1)
    q = queries.reshape(tokens, kv_here, per_kv, HD)
    keys = lax.all_gather(own_keys, "ctx", axis=0, tiled=True).reshape(-1, kv_here, HD)
    values = lax.all_gather(own_values, "ctx", axis=0, tiled=True).reshape(-1, kv_here, HD)
    docs = lax.all_gather(documents, "ctx", axis=0, tiled=True)
    q_pos = lax.axis_index("ctx") * tokens + jnp.arange(tokens, dtype=jnp.int32)
    k_pos = jnp.arange(keys.shape[0], dtype=jnp.int32)
    allowed = (k_pos[None, :] <= q_pos[:, None]) & (docs[None, :] == documents[:, None])
    scores = jnp.einsum("tghd,ngd->ghtn", q, keys, preferred_element_type=F32) / math.sqrt(HD)
    row_max = jnp.max(jnp.where(allowed, scores, -1e30), axis=3, keepdims=True)
    weights = jnp.where(allowed, jnp.exp(scores - row_max), 0.0)
    total = jnp.transpose(jnp.sum(weights, axis=3), (2, 0, 1))[..., None]
    mixed = jnp.einsum("ghtn,ngd->tghd", weights.astype(BF16), values, preferred_element_type=F32)
    attended = (mixed / total).astype(BF16).reshape(tokens, heads_here * HD)
    gathered = lax.all_gather(attended, "ctx", axis=0, tiled=True)
    terms = jnp.dot(gathered, out_weight, preferred_element_type=F32).astype(BF16)
    terms = jnp.transpose(terms.reshape(ctx, tp, tokens // tp, -1), (1, 0, 2, 3))
    summed = lax.psum_scatter(terms, "tp", scatter_dimension=0, tiled=True)[0]
    return lax.all_to_all(summed, "ctx", split_axis=0, concat_axis=2, tiled=True)[0]


def solution(mesh):
    ctx, tp = mesh.shape["ctx"], mesh.shape["tp"]
    on_device = functools.partial(fused if (ctx, tp) == (8, 4) else general, ctx, tp)
    in_specs = (P("ctx", "tp"), P("ctx", None), P("ctx", None), P("ctx"), P("tp", "ctx"))
    return jax.shard_map(
        on_device, mesh=mesh, in_specs=in_specs,
        out_specs=P(("ctx", "tp"), None), check_vma=False,
    )
```

```python
import functools
import math

import jax
import jax.numpy as jnp
from jax import lax
from jax.experimental import pallas as pl
from jax.experimental.pallas import tpu as pltpu
from jax.sharding import PartitionSpec as P

HEADS = 64
KV_HEADS = 8
HD = 128
DOCS = 4
MESH = pl.DeviceIdType.MESH
F32 = jnp.float32
BF16 = jnp.bfloat16
SCALE2 = math.log2(math.e) / math.sqrt(HD)
UNITS = 4


def fused_kernel(
    q_ref, k_ref, v_ref, drow_ref, w_hbm, out_ref,
    w_ref, kv, docs, k_mask, q_mask, att, part, zin, fin,
    w_sem, kv_send, kv_recv, doc_send, doc_recv,
    att_send, att_recv, z_send, z_recv, x_send, x_recv,
):
    c = lax.axis_index("ctx")
    z = lax.axis_index("tp")
    ctx = kv.shape[0]
    tokens = q_ref.shape[0]
    rows = att.shape[2]
    kv_here = kv.shape[2] // (2 * HD)
    per_kv = q_ref.shape[1] // HD // kv_here
    unit = part.shape[3]
    width = UNITS * unit

    y, x, core = c // 4, (c // 2) % 2, c % 2

    def at(yy, xx, cc):
        return yy * 4 + xx * 2 + cc

    sib, xn, yn = at(y, x, 1 - core), at(y, 1 - x, core), at(1 - y, x, core)
    dg = at(1 - y, 1 - x, core)
    sib_xn, sib_yn = at(y, 1 - x, 1 - core), at(1 - y, x, 1 - core)
    sib_dg = at(1 - y, 1 - x, 1 - core)

    far = z // 2
    out = 1 - 2 * far
    mid = z * (1 - far) + (3 - z) * far
    ahead, behind = z + out, z - out

    def chunk(p):
        mirrored = (1 - mid) * (3 - p) + mid * (3, 0, 2, 1)[p]
        return mirrored * (1 - far) + (3 - mirrored) * far

    def remote(src, dst, ss, rs, device):
        return pltpu.make_async_remote_copy(
            src_ref=src, dst_ref=dst, send_sem=ss, recv_sem=rs,
            device_id=device, device_id_type=MESH,
        )

    w_copy = pltpu.make_async_copy(w_hbm, w_ref, w_sem)
    w_copy.start()

    barrier = pltpu.get_barrier_semaphore()
    for step in range(1, ctx):
        pl.semaphore_signal(
            barrier, inc=1, device_id=(lax.rem(c + step, ctx), z), device_id_type=MESH
        )
    pl.semaphore_signal(barrier, inc=1, device_id=(c, ahead), device_id_type=MESH)

    @pl.when(mid == 1)
    def _():
        pl.semaphore_signal(barrier, inc=1, device_id=(c, behind), device_id_type=MESH)

    first = pl.multiple_of(z * kv_here * HD, kv_here * HD)
    kv[c, :, : kv_here * HD] = k_ref[:, pl.ds(first, kv_here * HD)]
    kv[c, :, kv_here * HD :] = v_ref[:, pl.ds(first, kv_here * HD)]
    docs[c] = jnp.broadcast_to(drow_ref[...], docs.shape[1:])
    pl.semaphore_wait(barrier, ctx + mid)

    def moves(buf, ss, rs):
        half = buf.shape[1] // 2
        lower, upper = pl.ds(0, half), pl.ds(half, half)
        own = [
            remote(buf.at[c], buf.at[c], ss.at[0], rs.at[0], (sib, z)),
            remote(buf.at[c], buf.at[c], ss.at[1], rs.at[1], (xn, z)),
            remote(buf.at[c], buf.at[c], ss.at[2], rs.at[2], (yn, z)),
        ]
        fwd = [
            remote(buf.at[xn, lower], buf.at[xn, lower], ss.at[3], rs.at[3], (yn, z)),
            remote(buf.at[yn, upper], buf.at[yn, upper], ss.at[4], rs.at[4], (xn, z)),
            remote(buf.at[xn], buf.at[xn], ss.at[5], rs.at[5], (sib, z)),
            remote(buf.at[yn], buf.at[yn], ss.at[6], rs.at[6], (sib, z)),
            remote(buf.at[dg, lower], buf.at[dg, lower], ss.at[7], rs.at[7], (sib, z)),
            remote(buf.at[dg, upper], buf.at[dg, upper], ss.at[8], rs.at[8], (sib, z)),
        ]

        def got(n, view):
            remote(view, view, ss.at[n], rs.at[n], (sib, z)).wait_recv()

        def start_own():
            for copy in own:
                copy.start()

        def forward_near():
            got(1, buf.at[xn])
            fwd[0].start()
            fwd[2].start()
            got(2, buf.at[yn])
            fwd[1].start()
            fwd[3].start()

        def forward_diagonal():
            got(3, buf.at[dg, lower])
            fwd[4].start()
            got(4, buf.at[dg, upper])
            fwd[5].start()

        def all_in():
            got(0, buf.at[sib])
            got(5, buf.at[sib_xn])
            got(6, buf.at[sib_yn])
            got(7, buf.at[sib_dg, lower])
            got(8, buf.at[sib_dg, upper])

        def all_sent():
            for copy in own + fwd:
                copy.wait_send()

        return start_own, forward_near, forward_diagonal, all_in, all_sent

    kv_moves = moves(kv, kv_send, kv_recv)
    kv_moves[0]()
    doc_copies = []
    for step in range(1, ctx):
        peer = lax.rem(c + step, ctx)
        doc_copies.append(
            remote(docs.at[c], docs.at[c], doc_send.at[step], doc_recv.at[step], (peer, z))
        )
        doc_copies[-1].start()
    kv_moves[1]()
    kv_moves[2]()
    for step in range(1, ctx):
        source = lax.rem(c + ctx - step, ctx)
        remote(
            docs.at[source], docs.at[source], doc_send.at[step], doc_recv.at[step], (source, z)
        ).wait_recv()
    kv_moves[3]()

    lane = lax.broadcasted_iota(jnp.int32, (tokens, HD), 1)

    def down(slot):
        across = docs[slot][0:1, :].astype(F32)
        return jnp.broadcast_to(across, (HD, tokens)).T.astype(jnp.int32)

    q_mask[...] = jnp.where(lane == down(c), 1.0, 0.0).astype(BF16)

    def mask_slot(slot, _):
        apart = (lane < DOCS) & (lane != down(slot))
        k_mask[slot] = jnp.where(apart, -(2.0**100), 0.0).astype(BF16)
        return 0

    lax.fori_loop(0, ctx, mask_slot, 0)

    pair = 2
    keys = pair * tokens
    blocks = c // pair

    def attend(p):
        t = chunk(p)
        begin = pl.multiple_of(t * rows, rows)
        q_extra = q_mask[pl.ds(begin, rows), :]
        qs = [
            jnp.concatenate(
                [
                    jnp.concatenate(
                        [
                            q_ref[
                                pl.ds(begin, rows),
                                (g * per_kv + h) * HD : (g * per_kv + h + 1) * HD,
                            ],
                            q_extra,
                        ],
                        axis=1,
                    )
                    for h in range(per_kv)
                ],
                axis=0,
            )
            for g in range(kv_here)
        ]

        def body(b, carry, bias=None):
            here = pl.ds(pair * b, pair)
            extra = k_mask[here].reshape(keys, HD)
            ones = jnp.ones((keys, HD), BF16)
            state = []
            for g in range(kv_here):
                old_max, acc = carry[g]
                k = kv[here, :, g * HD : (g + 1) * HD].reshape(keys, HD)
                v = kv[here, :, (kv_here + g) * HD : (kv_here + g + 1) * HD].reshape(keys, HD)
                s = lax.dot_general(
                    qs[g], jnp.concatenate([k, extra], axis=1), (((1,), (1,)), ((), ())),
                    preferred_element_type=F32,
                ) * SCALE2
                if bias is not None:
                    s = (s.reshape(per_kv, rows, keys) + bias[None]).reshape(per_kv * rows, keys)
                new_max = jnp.maximum(old_max, jnp.max(s, axis=1, keepdims=True))
                weights = jnp.exp2(s - new_max).astype(BF16)
                acc = acc * jnp.exp2(old_max - new_max) + jnp.dot(
                    weights, jnp.concatenate([v, ones], axis=1), preferred_element_type=F32
                )
                state.append((new_max, acc))
            return tuple(state)

        state = lax.fori_loop(
            0,
            blocks,
            body,
            (
                (
                    jnp.full((per_kv * rows, 1), -1e30, F32),
                    jnp.zeros((per_kv * rows, 2 * HD), F32),
                ),
            )
            * kv_here,
        )
        q_pos = c * tokens + t * rows + lax.broadcasted_iota(jnp.int32, (rows, keys), 0)
        k_pos = blocks * keys + lax.broadcasted_iota(jnp.int32, (rows, keys), 1)
        state = body(blocks, state, jnp.where(k_pos <= q_pos, 0.0, -1e30).astype(F32))
        for g in range(kv_here):
            acc = state[g][1]
            o = (acc[:, :HD] / acc[:, HD:]).astype(BF16)
            for h in range(per_kv):
                att[p, c, :, (g * per_kv + h) * HD : (g * per_kv + h + 1) * HD] = o[
                    h * rows : (h + 1) * rows
                ]

    def end_hop(p, j):
        return remote(
            part.at[p, j], zin.at[(0, 2, 3)[p], j], z_send.at[p, j],
            z_recv.at[(0, 2, 3)[p], j], (c, ahead),
        )

    def mid_hop(p, j):
        return remote(
            part.at[p, j], zin.at[(1, 0, 4)[p], j], z_send.at[p, j],
            z_recv.at[(1, 0, 4)[p], j], (c, (ahead, behind, ahead)[p]),
        )

    def z_got(slot, j):
        remote(
            zin.at[slot, j], zin.at[slot, j], z_send.at[0, j], z_recv.at[slot, j], (c, ahead)
        ).wait_recv()

    def project(p):
        def body(j, _):
            a = att[p].reshape(ctx * rows, att.shape[3])
            w = w_ref[:, pl.ds(pl.multiple_of(j * unit, unit), unit)]
            part[p, j] = jnp.dot(a, w, preferred_element_type=F32).astype(BF16)
            if p < 3:
                @pl.when(mid == 0)
                def _():
                    end_hop(p, j).start()

            return 0

        lax.fori_loop(0, UNITS, body, 0)

    def pass_on(*units):
        @pl.when(mid == 1)
        def _():
            for p, j in units:
                z_got(p, j)
                part[p, j] = (part[p, j].astype(F32) + zin[p, j].astype(F32)).astype(BF16)
                mid_hop(p, j).start()

    w_copy.wait()
    steps = [
        moves(att.at[p], att_send.at[p], att_recv.at[p]) for p in range(4)
    ]
    attend(0)
    steps[0][0]()
    steps[0][1]()
    steps[0][2]()
    steps[0][3]()
    project(0)
    attend(1)
    steps[1][0]()
    pass_on((0, 0))
    steps[1][1]()
    steps[1][2]()
    pass_on((0, 1))
    attend(2)
    steps[1][3]()
    steps[2][0]()
    project(1)
    pass_on((0, 2), (1, 0))
    steps[2][1]()
    steps[2][2]()
    pass_on((0, 3), (1, 1))
    attend(3)
    steps[2][3]()
    steps[3][0]()
    project(2)
    pass_on((1, 2))
    steps[3][1]()
    steps[3][2]()
    pass_on((1, 3))
    steps[3][3]()
    project(3)
    pass_on((2, 0), (2, 1), (2, 2), (2, 3))

    x_copies = []
    for j in range(UNITS):
        @pl.when(mid == 0)
        def _():
            z_got(0, j)
            total = part[3, j].astype(F32) + zin[0, j].astype(F32)
            fin[j] = total.astype(BF16).reshape(fin.shape[1:])

        @pl.when(mid == 1)
        def _():
            z_got(4, j)
            z_got(3, j)
            total = part[3, j].astype(F32) + zin[3, j].astype(F32) + zin[4, j].astype(F32)
            fin[j] = total.astype(BF16).reshape(fin.shape[1:])

        columns = pl.ds(pl.multiple_of(c * width + j * unit, unit), unit)
        for step in range(1, ctx):
            peer = lax.rem(c + step, ctx)
            x_copies.append(
                remote(
                    fin.at[j, peer], out_ref.at[:, columns], x_send.at[step, j],
                    x_recv.at[step, j], (peer, z),
                )
            )
            x_copies[-1].start()
        out_ref[:, columns] = fin[j, c]

    for j in range(UNITS):
        for step in range(1, ctx):
            source = lax.rem(c + ctx - step, ctx)
            columns = pl.ds(pl.multiple_of(source * width + j * unit, unit), unit)
            remote(
                fin.at[j, source], out_ref.at[:, columns], x_send.at[step, j],
                x_recv.at[step, j], (source, z),
            ).wait_recv()

    kv_moves[4]()
    for copy in doc_copies + x_copies:
        copy.wait_send()
    for step in steps:
        step[4]()

    @pl.when(mid == 0)
    def _():
        for p in range(3):
            for j in range(UNITS):
                end_hop(p, j).wait_send()

    @pl.when(mid == 1)
    def _():
        for p in range(3):
            for j in range(UNITS):
                mid_hop(p, j).wait_send()


def fused(ctx, tp, queries, key_rows, value_rows, documents, out_weight):
    tokens, heads_width = queries.shape
    kv_here = heads_width // HD // (HEADS // KV_HEADS)
    rows = tokens // tp
    depth, width = out_weight.shape
    unit = width // UNITS
    vmem = pl.BlockSpec(memory_space=pltpu.VMEM)
    dma = pltpu.SemaphoreType.DMA
    return pl.pallas_call(
        fused_kernel,
        out_shape=jax.ShapeDtypeStruct((rows, width * ctx), BF16),
        in_specs=[vmem] * 4 + [pl.BlockSpec(memory_space=pl.ANY)],
        out_specs=vmem,
        scratch_shapes=[
            pltpu.VMEM((depth, width), BF16),
            pltpu.VMEM((ctx, tokens, 2 * kv_here * HD), BF16),
            pltpu.VMEM((ctx, 8, tokens), jnp.int32),
            pltpu.VMEM((ctx, tokens, HD), BF16),
            pltpu.VMEM((tokens, HD), BF16),
            pltpu.VMEM((tp, ctx, rows, heads_width), BF16),
            pltpu.VMEM((tp, UNITS, ctx * rows, unit), BF16),
            pltpu.VMEM((5, UNITS, ctx * rows, unit), BF16),
            pltpu.VMEM((UNITS, ctx, rows, unit), BF16),
            dma,
            dma((9,)),
            dma((9,)),
            dma((ctx,)),
            dma((ctx,)),
            dma((tp, 9)),
            dma((tp, 9)),
            dma((3, UNITS)),
            dma((5, UNITS)),
            dma((ctx, UNITS)),
            dma((ctx, UNITS)),
        ],
        compiler_params=pltpu.CompilerParams(
            collective_id=0, has_side_effects=True, vmem_limit_bytes=56 * 1024 * 1024
        ),
    )(
        queries, key_rows, value_rows, documents.reshape(1, tokens), out_weight,
    )


def general(ctx, tp, queries, key_rows, value_rows, documents, out_weight):
    tokens = queries.shape[0]
    heads_here = queries.shape[1] // HD
    group_size = HEADS // KV_HEADS
    kv_here = max(1, heads_here // group_size)
    per_kv = heads_here // kv_here
    kv_first = lax.axis_index("tp") * heads_here // group_size
    own_keys = lax.dynamic_slice_in_dim(key_rows, kv_first * HD, kv_here * HD, 1)
    own_values = lax.dynamic_slice_in_dim(value_rows, kv_first * HD, kv_here * HD, 1)
    q = queries.reshape(tokens, kv_here, per_kv, HD)
    keys = lax.all_gather(own_keys, "ctx", axis=0, tiled=True).reshape(-1, kv_here, HD)
    values = lax.all_gather(own_values, "ctx", axis=0, tiled=True).reshape(-1, kv_here, HD)
    docs = lax.all_gather(documents, "ctx", axis=0, tiled=True)
    q_pos = lax.axis_index("ctx") * tokens + jnp.arange(tokens, dtype=jnp.int32)
    k_pos = jnp.arange(keys.shape[0], dtype=jnp.int32)
    allowed = (k_pos[None, :] <= q_pos[:, None]) & (docs[None, :] == documents[:, None])
    scores = jnp.einsum("tghd,ngd->ghtn", q, keys, preferred_element_type=F32) / math.sqrt(HD)
    row_max = jnp.max(jnp.where(allowed, scores, -1e30), axis=3, keepdims=True)
    weights = jnp.where(allowed, jnp.exp(scores - row_max), 0.0)
    total = jnp.transpose(jnp.sum(weights, axis=3), (2, 0, 1))[..., None]
    mixed = jnp.einsum("ghtn,ngd->tghd", weights.astype(BF16), values, preferred_element_type=F32)
    attended = (mixed / total).astype(BF16).reshape(tokens, heads_here * HD)
    gathered = lax.all_gather(attended, "ctx", axis=0, tiled=True)
    terms = jnp.dot(gathered, out_weight, preferred_element_type=F32).astype(BF16)
    terms = jnp.transpose(terms.reshape(ctx, tp, tokens // tp, -1), (1, 0, 2, 3))
    summed = lax.psum_scatter(terms, "tp", scatter_dimension=0, tiled=True)[0]
    return lax.all_to_all(summed, "ctx", split_axis=0, concat_axis=2, tiled=True)[0]


def solution(mesh):
    ctx, tp = mesh.shape["ctx"], mesh.shape["tp"]
    on_device = functools.partial(fused if (ctx, tp) == (8, 4) else general, ctx, tp)
    in_specs = (P("ctx", "tp"), P("ctx", None), P("ctx", None), P("ctx"), P("tp", "ctx"))
    return jax.shard_map(
        on_device, mesh=mesh, in_specs=in_specs,
        out_specs=P(("ctx", "tp"), None), check_vma=False,
    )
```

```python
import functools
import math

import jax
import jax.numpy as jnp
from jax import lax
from jax.experimental import pallas as pl
from jax.experimental.pallas import tpu as pltpu
from jax.sharding import PartitionSpec as P

HEADS = 64
KV_HEADS = 8
HD = 128
DOCS = 4
MESH = pl.DeviceIdType.MESH
F32 = jnp.float32
BF16 = jnp.bfloat16
SCALE2 = math.log2(math.e) / math.sqrt(HD)
UNITS = 4


def fused_kernel(
    q_ref, k_ref, v_ref, drow_ref, w_hbm, out_ref,
    w_ref, kv, docs, k_mask, q_mask, att, part, row_part, z_cols, z_rows, fin,
    w_sem, kv_send, kv_recv, doc_send, doc_recv,
    att_send, att_recv, z_send, z_recv, x_send, x_recv,
):
    c = lax.axis_index("ctx")
    z = lax.axis_index("tp")
    ctx = kv.shape[0]
    tokens = q_ref.shape[0]
    rows = att.shape[2]
    kv_here = kv.shape[2] // (2 * HD)
    per_kv = q_ref.shape[1] // HD // kv_here
    unit = part.shape[3]
    width = UNITS * unit

    y, x, core = c // 4, (c // 2) % 2, c % 2

    def at(yy, xx, cc):
        return yy * 4 + xx * 2 + cc

    sib, xn, yn = at(y, x, 1 - core), at(y, 1 - x, core), at(1 - y, x, core)
    dg = at(1 - y, 1 - x, core)
    sib_xn, sib_yn = at(y, 1 - x, 1 - core), at(1 - y, x, 1 - core)
    sib_dg = at(1 - y, 1 - x, 1 - core)

    far = z // 2
    out = 1 - 2 * far
    mid = z * (1 - far) + (3 - z) * far
    ahead, behind = z + out, z - out

    def chunk(p):
        mirrored = (1 - mid) * (3 - p) + mid * (3, 0, 2, 1)[p]
        return mirrored * (1 - far) + (3 - mirrored) * far

    def remote(src, dst, ss, rs, device):
        return pltpu.make_async_remote_copy(
            src_ref=src, dst_ref=dst, send_sem=ss, recv_sem=rs,
            device_id=device, device_id_type=MESH,
        )

    w_copy = pltpu.make_async_copy(w_hbm, w_ref, w_sem)
    w_copy.start()

    barrier = pltpu.get_barrier_semaphore()
    for step in range(1, ctx):
        pl.semaphore_signal(
            barrier, inc=1, device_id=(lax.rem(c + step, ctx), z), device_id_type=MESH
        )
    pl.semaphore_signal(barrier, inc=1, device_id=(c, ahead), device_id_type=MESH)

    @pl.when(mid == 1)
    def _():
        pl.semaphore_signal(barrier, inc=1, device_id=(c, behind), device_id_type=MESH)

    first = pl.multiple_of(z * kv_here * HD, kv_here * HD)
    kv[c, :, : kv_here * HD] = k_ref[:, pl.ds(first, kv_here * HD)]
    kv[c, :, kv_here * HD :] = v_ref[:, pl.ds(first, kv_here * HD)]
    docs[c] = jnp.broadcast_to(drow_ref[...], docs.shape[1:])
    pl.semaphore_wait(barrier, ctx + mid)

    def moves(buf, ss, rs):
        half = buf.shape[1] // 2
        lower, upper = pl.ds(0, half), pl.ds(half, half)
        own = [
            remote(buf.at[c], buf.at[c], ss.at[0], rs.at[0], (sib, z)),
            remote(buf.at[c], buf.at[c], ss.at[1], rs.at[1], (xn, z)),
            remote(buf.at[c], buf.at[c], ss.at[2], rs.at[2], (yn, z)),
        ]
        fwd = [
            remote(buf.at[xn, lower], buf.at[xn, lower], ss.at[3], rs.at[3], (yn, z)),
            remote(buf.at[yn, upper], buf.at[yn, upper], ss.at[4], rs.at[4], (xn, z)),
            remote(buf.at[xn], buf.at[xn], ss.at[5], rs.at[5], (sib, z)),
            remote(buf.at[yn], buf.at[yn], ss.at[6], rs.at[6], (sib, z)),
            remote(buf.at[dg, lower], buf.at[dg, lower], ss.at[7], rs.at[7], (sib, z)),
            remote(buf.at[dg, upper], buf.at[dg, upper], ss.at[8], rs.at[8], (sib, z)),
        ]

        def got(n, view):
            remote(view, view, ss.at[n], rs.at[n], (sib, z)).wait_recv()

        def start_own():
            for copy in own:
                copy.start()

        def own_in():
            got(0, buf.at[sib])

        def from_x():
            got(1, buf.at[xn])
            fwd[0].start()
            fwd[2].start()

        def from_y():
            got(2, buf.at[yn])
            fwd[1].start()
            fwd[3].start()

        def from_diagonal():
            got(3, buf.at[dg, lower])
            fwd[4].start()
            got(4, buf.at[dg, upper])
            fwd[5].start()

        def x_in():
            got(5, buf.at[sib_xn])

        def y_in():
            got(6, buf.at[sib_yn])

        def diagonal_in():
            got(7, buf.at[sib_dg, lower])
            got(8, buf.at[sib_dg, upper])

        def all_sent():
            for copy in own + fwd:
                copy.wait_send()

        def near():
            from_x()
            from_y()

        def all_in():
            own_in()
            x_in()
            y_in()
            diagonal_in()

        return dict(locals())

    kv_moves = moves(kv, kv_send, kv_recv)
    doc_copies = []
    for step in range(1, ctx):
        peer = lax.rem(c + step, ctx)
        doc_copies.append(
            remote(docs.at[c], docs.at[c], doc_send.at[step], doc_recv.at[step], (peer, z))
        )
        doc_copies[-1].start()
    kv_moves["start_own"]()
    for step in range(1, ctx):
        source = lax.rem(c + ctx - step, ctx)
        remote(
            docs.at[source], docs.at[source], doc_send.at[step], doc_recv.at[step], (source, z)
        ).wait_recv()

    lane = lax.broadcasted_iota(jnp.int32, (tokens, HD), 1)

    def down(slot):
        across = docs[slot][0:1, :].astype(F32)
        return jnp.broadcast_to(across, (HD, tokens)).T.astype(jnp.int32)

    q_mask[...] = jnp.where(lane == down(c), 1.0, 0.0).astype(BF16)

    def mask_slot(slot, _):
        apart = (lane < DOCS) & (lane != down(slot))
        k_mask[slot] = jnp.where(apart, -(2.0**100), 0.0).astype(BF16)
        return 0

    lax.fori_loop(0, ctx, mask_slot, 0)

    pair = 2
    keys = pair * tokens
    blocks = c // pair

    def attend(p):
        t = chunk(p)
        begin = pl.multiple_of(t * rows, rows)
        q_extra = q_mask[pl.ds(begin, rows), :]
        qs = [
            jnp.concatenate(
                [
                    jnp.concatenate(
                        [
                            q_ref[
                                pl.ds(begin, rows),
                                (g * per_kv + h) * HD : (g * per_kv + h + 1) * HD,
                            ],
                            q_extra,
                        ],
                        axis=1,
                    )
                    for h in range(per_kv)
                ],
                axis=0,
            )
            for g in range(kv_here)
        ]

        def body(b, carry, bias=None):
            here = pl.ds(pair * b, pair)
            extra = k_mask[here].reshape(keys, HD)
            ones = jnp.ones((keys, HD), BF16)
            state = []
            for g in range(kv_here):
                old_max, acc = carry[g]
                k = kv[here, :, g * HD : (g + 1) * HD].reshape(keys, HD)
                v = kv[here, :, (kv_here + g) * HD : (kv_here + g + 1) * HD].reshape(keys, HD)
                s = lax.dot_general(
                    qs[g], jnp.concatenate([k, extra], axis=1), (((1,), (1,)), ((), ())),
                    preferred_element_type=F32,
                ) * SCALE2
                if bias is not None:
                    s = (s.reshape(per_kv, rows, keys) + bias[None]).reshape(per_kv * rows, keys)
                new_max = jnp.maximum(old_max, jnp.max(s, axis=1, keepdims=True))
                weights = jnp.exp2(s - new_max).astype(BF16)
                acc = acc * jnp.exp2(old_max - new_max) + jnp.dot(
                    weights, jnp.concatenate([v, ones], axis=1), preferred_element_type=F32
                )
                state.append((new_max, acc))
            return tuple(state)

        state = lax.fori_loop(
            0,
            blocks,
            body,
            (
                (
                    jnp.full((per_kv * rows, 1), -1e30, F32),
                    jnp.zeros((per_kv * rows, 2 * HD), F32),
                ),
            )
            * kv_here,
        )
        q_pos = c * tokens + t * rows + lax.broadcasted_iota(jnp.int32, (rows, keys), 0)
        k_pos = blocks * keys + lax.broadcasted_iota(jnp.int32, (rows, keys), 1)
        state = body(blocks, state, jnp.where(k_pos <= q_pos, 0.0, -1e30).astype(F32))
        for g in range(kv_here):
            acc = state[g][1]
            o = (acc[:, :HD] / acc[:, HD:]).astype(BF16)
            for h in range(per_kv):
                att[p, c, :, (g * per_kv + h) * HD : (g * per_kv + h + 1) * HD] = o[
                    h * rows : (h + 1) * rows
                ]

    def hop(src, dst, p, j, slot, to):
        return remote(src, dst, z_send.at[p, j], z_recv.at[slot, j], (c, to))

    def end_hop(p, j):
        if p == 0:
            return hop(row_part.at[0, j], z_rows.at[0, j], 0, j, 0, ahead)
        return hop(part.at[p - 1, j], z_cols.at[p - 1, j], p, j, p + 1, ahead)

    def mid_hop(p, j):
        if p == 2:
            return hop(part.at[1, j], z_cols.at[2, j], 2, j, 4, ahead)
        return hop(
            row_part.at[p, j], z_rows.at[1 - p, j], p, j, 1 - p, (ahead, behind)[p]
        )

    def z_got(slot, j):
        view = z_rows.at[slot, j] if slot < 2 else z_cols.at[slot - 2, j]
        remote(view, view, z_send.at[0, j], z_recv.at[slot, j], (c, ahead)).wait_recv()

    def project_rows(j):
        pick = pl.ds(j * (ctx // UNITS), ctx // UNITS)
        a = att[0, pick].reshape(ctx // UNITS * rows, att.shape[3])
        row_part[0, j] = jnp.dot(a, w_ref[...], preferred_element_type=F32).astype(BF16)

        @pl.when(mid == 0)
        def _():
            end_hop(0, j).start()

    def project(p):
        def body(j, _):
            a = att[p].reshape(ctx * rows, att.shape[3])
            columns = pl.ds(pl.multiple_of(j * unit, unit), unit)
            r = jnp.dot(a, w_ref[:, columns], preferred_element_type=F32).astype(BF16)
            in_rows = (2, 1, 2, 0)[p]

            @pl.when(mid != in_rows)
            def _():
                part[p - 1, j] = r

            if p < 3:
                @pl.when(mid == 0)
                def _():
                    end_hop(p, j).start()

            @pl.when(mid == in_rows)
            def _():
                row_part[1, :, :, columns] = r.reshape(UNITS, -1, unit)

            return 0

        lax.fori_loop(0, UNITS, body, 0)

    def pass_on(*units):
        @pl.when(mid == 1)
        def _():
            for p, j in units:
                z_got(p, j)
                mine = part.at[1, j] if p == 2 else row_part.at[p, j]
                theirs = z_cols.at[0, j] if p == 2 else z_rows.at[p, j]
                mine[...] = (mine[...].astype(F32) + theirs[...].astype(F32)).astype(BF16)
                mid_hop(p, j).start()

    steps = [
        moves(att.at[p], att_send.at[p], att_recv.at[p]) for p in range(4)
    ]
    chip = 2 * y + x
    kv_moves["own_in"]()

    def phase(i, _):
        @pl.when(i == 1)
        def _():
            kv_moves["near"]()
            kv_moves["x_in"]()

        @pl.when(i == 2)
        def _():
            kv_moves["from_diagonal"]()
            kv_moves["y_in"]()
            kv_moves["diagonal_in"]()

        @pl.when((chip == i) | ((i == 2) & (chip == 3)))
        def _():
            attend(0)
            steps[0]["start_own"]()

        return 0

    lax.fori_loop(0, 3, phase, 0)
    w_copy.wait()
    for j in range(UNITS):
        @pl.when(chip == j)
        def _():
            steps[0]["own_in"]()

        @pl.when(2 * y + 1 - x == j)
        def _():
            steps[0]["from_x"]()
            steps[0]["x_in"]()

        @pl.when(2 * (1 - y) + x == j)
        def _():
            steps[0]["from_y"]()
            steps[0]["y_in"]()

        @pl.when(2 * (1 - y) + 1 - x == j)
        def _():
            steps[0]["from_diagonal"]()
            steps[0]["diagonal_in"]()

        project_rows(j)
        if j == 1:
            attend(1)
            steps[1]["start_own"]()

    attend(2)
    steps[1]["near"]()
    steps[2]["start_own"]()
    steps[1]["from_diagonal"]()
    steps[1]["all_in"]()
    project(1)
    pass_on((0, 0))
    steps[2]["near"]()
    attend(3)
    steps[3]["start_own"]()
    steps[2]["from_diagonal"]()
    steps[2]["all_in"]()
    project(2)
    pass_on((0, 1), (0, 2))
    steps[3]["near"]()
    steps[3]["from_diagonal"]()
    steps[3]["all_in"]()
    project(3)
    pass_on(
        (0, 3), (1, 0), (1, 1), (1, 2), (2, 0), (1, 3), (2, 1), (2, 2), (2, 3)
    )

    @pl.when(mid == 0)
    def _():
        for j in range(UNITS):
            z_got(0, j)
            total = (row_part[1, j].astype(F32) + z_rows[0, j].astype(F32)).astype(BF16)
            pair_of = ctx // UNITS
            for n in range(UNITS):
                fin[n, pair_of * j : pair_of * (j + 1)] = total[
                    :, n * unit : (n + 1) * unit
                ].reshape(pair_of, rows, unit)

    x_copies = []
    for j in range(UNITS):
        @pl.when(mid == 1)
        def _():
            z_got(4, j)
            z_got(3, j)
            total = part[2, j].astype(F32) + z_cols[1, j].astype(F32) + z_cols[2, j].astype(F32)
            fin[j] = total.astype(BF16).reshape(fin.shape[1:])

        columns = pl.ds(pl.multiple_of(c * width + j * unit, unit), unit)
        for step in range(1, ctx):
            peer = lax.rem(c + step, ctx)
            x_copies.append(
                remote(
                    fin.at[j, peer], out_ref.at[:, columns], x_send.at[step, j],
                    x_recv.at[step, j], (peer, z),
                )
            )
            x_copies[-1].start()
        out_ref[:, columns] = fin[j, c]

    for j in range(UNITS):
        for step in range(1, ctx):
            source = lax.rem(c + ctx - step, ctx)
            columns = pl.ds(pl.multiple_of(source * width + j * unit, unit), unit)
            remote(
                fin.at[j, source], out_ref.at[:, columns], x_send.at[step, j],
                x_recv.at[step, j], (source, z),
            ).wait_recv()

    kv_moves["all_sent"]()
    for copy in doc_copies + x_copies:
        copy.wait_send()
    for step in steps:
        step["all_sent"]()

    @pl.when(mid == 0)
    def _():
        for p in range(3):
            for j in range(UNITS):
                end_hop(p, j).wait_send()

    @pl.when(mid == 1)
    def _():
        for p in range(3):
            for j in range(UNITS):
                mid_hop(p, j).wait_send()


def fused(ctx, tp, queries, key_rows, value_rows, documents, out_weight):
    tokens, heads_width = queries.shape
    kv_here = heads_width // HD // (HEADS // KV_HEADS)
    rows = tokens // tp
    depth, width = out_weight.shape
    unit = width // UNITS
    vmem = pl.BlockSpec(memory_space=pltpu.VMEM)
    dma = pltpu.SemaphoreType.DMA
    return pl.pallas_call(
        fused_kernel,
        out_shape=jax.ShapeDtypeStruct((rows, width * ctx), BF16),
        in_specs=[vmem] * 4 + [pl.BlockSpec(memory_space=pl.ANY)],
        out_specs=vmem,
        scratch_shapes=[
            pltpu.VMEM((depth, width), BF16),
            pltpu.VMEM((ctx, tokens, 2 * kv_here * HD), BF16),
            pltpu.VMEM((ctx, 8, tokens), jnp.int32),
            pltpu.VMEM((ctx, tokens, HD), BF16),
            pltpu.VMEM((tokens, HD), BF16),
            pltpu.VMEM((tp, ctx, rows, heads_width), BF16),
            pltpu.VMEM((3, UNITS, ctx * rows, unit), BF16),
            pltpu.VMEM((2, UNITS, ctx * rows // UNITS, width), BF16),
            pltpu.VMEM((3, UNITS, ctx * rows, unit), BF16),
            pltpu.VMEM((2, UNITS, ctx * rows // UNITS, width), BF16),
            pltpu.VMEM((UNITS, ctx, rows, unit), BF16),
            dma,
            dma((9,)),
            dma((9,)),
            dma((ctx,)),
            dma((ctx,)),
            dma((tp, 9)),
            dma((tp, 9)),
            dma((3, UNITS)),
            dma((5, UNITS)),
            dma((ctx, UNITS)),
            dma((ctx, UNITS)),
        ],
        compiler_params=pltpu.CompilerParams(
            collective_id=0, has_side_effects=True, vmem_limit_bytes=56 * 1024 * 1024
        ),
    )(
        queries, key_rows, value_rows, documents.reshape(1, tokens), out_weight,
    )


def general(ctx, tp, queries, key_rows, value_rows, documents, out_weight):
    tokens = queries.shape[0]
    heads_here = queries.shape[1] // HD
    group_size = HEADS // KV_HEADS
    kv_here = max(1, heads_here // group_size)
    per_kv = heads_here // kv_here
    kv_first = lax.axis_index("tp") * heads_here // group_size
    own_keys = lax.dynamic_slice_in_dim(key_rows, kv_first * HD, kv_here * HD, 1)
    own_values = lax.dynamic_slice_in_dim(value_rows, kv_first * HD, kv_here * HD, 1)
    q = queries.reshape(tokens, kv_here, per_kv, HD)
    keys = lax.all_gather(own_keys, "ctx", axis=0, tiled=True).reshape(-1, kv_here, HD)
    values = lax.all_gather(own_values, "ctx", axis=0, tiled=True).reshape(-1, kv_here, HD)
    docs = lax.all_gather(documents, "ctx", axis=0, tiled=True)
    q_pos = lax.axis_index("ctx") * tokens + jnp.arange(tokens, dtype=jnp.int32)
    k_pos = jnp.arange(keys.shape[0], dtype=jnp.int32)
    allowed = (k_pos[None, :] <= q_pos[:, None]) & (docs[None, :] == documents[:, None])
    scores = jnp.einsum("tghd,ngd->ghtn", q, keys, preferred_element_type=F32) / math.sqrt(HD)
    row_max = jnp.max(jnp.where(allowed, scores, -1e30), axis=3, keepdims=True)
    weights = jnp.where(allowed, jnp.exp(scores - row_max), 0.0)
    total = jnp.transpose(jnp.sum(weights, axis=3), (2, 0, 1))[..., None]
    mixed = jnp.einsum("ghtn,ngd->tghd", weights.astype(BF16), values, preferred_element_type=F32)
    attended = (mixed / total).astype(BF16).reshape(tokens, heads_here * HD)
    gathered = lax.all_gather(attended, "ctx", axis=0, tiled=True)
    terms = jnp.dot(gathered, out_weight, preferred_element_type=F32).astype(BF16)
    terms = jnp.transpose(terms.reshape(ctx, tp, tokens // tp, -1), (1, 0, 2, 3))
    summed = lax.psum_scatter(terms, "tp", scatter_dimension=0, tiled=True)[0]
    return lax.all_to_all(summed, "ctx", split_axis=0, concat_axis=2, tiled=True)[0]


def solution(mesh):
    ctx, tp = mesh.shape["ctx"], mesh.shape["tp"]
    on_device = functools.partial(fused if (ctx, tp) == (8, 4) else general, ctx, tp)
    in_specs = (P("ctx", "tp"), P("ctx", None), P("ctx", None), P("ctx"), P("tp", "ctx"))
    return jax.shard_map(
        on_device, mesh=mesh, in_specs=in_specs,
        out_specs=P(("ctx", "tp"), None), check_vma=False,
    )
```

```python
import functools
import math

import jax
import jax.numpy as jnp
from jax import lax
from jax.experimental import pallas as pl
from jax.experimental.pallas import tpu as pltpu
from jax.sharding import PartitionSpec as P

HEADS = 64
KV_HEADS = 8
HD = 128
DOCS = 4
MESH = pl.DeviceIdType.MESH
F32 = jnp.float32
BF16 = jnp.bfloat16
SCALE2 = math.log2(math.e) / math.sqrt(HD)
UNITS = 4


def fused_kernel(
    q_ref, k_ref, v_ref, drow_ref, w_hbm, out_ref,
    w_ref, kv, docs, k_mask, q_mask, v_down, att, part, zin, fin,
    w_sem, kv_send, kv_recv, doc_send, doc_recv,
    att_send, att_recv, z_send, z_recv, x_send, x_recv,
):
    c = lax.axis_index("ctx")
    z = lax.axis_index("tp")
    ctx = kv.shape[0]
    tokens = q_ref.shape[0]
    rows = att.shape[2]
    kv_here = kv.shape[2] // (2 * HD)
    per_kv = q_ref.shape[1] // HD // kv_here
    unit = part.shape[3]
    width = UNITS * unit

    y, x, core = c // 4, (c // 2) % 2, c % 2

    def at(yy, xx, cc):
        return yy * 4 + xx * 2 + cc

    sib, xn, yn = at(y, x, 1 - core), at(y, 1 - x, core), at(1 - y, x, core)
    dg = at(1 - y, 1 - x, core)
    sib_xn, sib_yn = at(y, 1 - x, 1 - core), at(1 - y, x, 1 - core)
    sib_dg = at(1 - y, 1 - x, 1 - core)

    far = z // 2
    out = 1 - 2 * far
    mid = z * (1 - far) + (3 - z) * far
    ahead, behind = z + out, z - out

    def chunk(p):
        mirrored = (1 - mid) * (3 - p) + mid * (3, 0, 2, 1)[p]
        return mirrored * (1 - far) + (3 - mirrored) * far

    def remote(src, dst, ss, rs, device):
        return pltpu.make_async_remote_copy(
            src_ref=src, dst_ref=dst, send_sem=ss, recv_sem=rs,
            device_id=device, device_id_type=MESH,
        )

    w_copy = pltpu.make_async_copy(w_hbm, w_ref, w_sem)
    w_copy.start()

    barrier = pltpu.get_barrier_semaphore()
    for step in range(1, ctx):
        pl.semaphore_signal(
            barrier, inc=1, device_id=(lax.rem(c + step, ctx), z), device_id_type=MESH
        )
    pl.semaphore_signal(barrier, inc=1, device_id=(c, ahead), device_id_type=MESH)

    @pl.when(mid == 1)
    def _():
        pl.semaphore_signal(barrier, inc=1, device_id=(c, behind), device_id_type=MESH)

    first = pl.multiple_of(z * kv_here * HD, kv_here * HD)
    kv[c, :, : kv_here * HD] = k_ref[:, pl.ds(first, kv_here * HD)]
    kv[c, :, kv_here * HD :] = v_ref[:, pl.ds(first, kv_here * HD)]
    docs[c] = jnp.broadcast_to(drow_ref[...], docs.shape[1:])
    pl.semaphore_wait(barrier, ctx + mid)

    def moves(buf, ss, rs):
        half = buf.shape[1] // 2
        lower, upper = pl.ds(0, half), pl.ds(half, half)
        own = [
            remote(buf.at[c], buf.at[c], ss.at[0], rs.at[0], (sib, z)),
            remote(buf.at[c], buf.at[c], ss.at[1], rs.at[1], (xn, z)),
            remote(buf.at[c], buf.at[c], ss.at[2], rs.at[2], (yn, z)),
        ]
        fwd = [
            remote(buf.at[xn, lower], buf.at[xn, lower], ss.at[3], rs.at[3], (yn, z)),
            remote(buf.at[yn, upper], buf.at[yn, upper], ss.at[4], rs.at[4], (xn, z)),
            remote(buf.at[xn], buf.at[xn], ss.at[5], rs.at[5], (sib, z)),
            remote(buf.at[yn], buf.at[yn], ss.at[6], rs.at[6], (sib, z)),
            remote(buf.at[dg, lower], buf.at[dg, lower], ss.at[7], rs.at[7], (sib, z)),
            remote(buf.at[dg, upper], buf.at[dg, upper], ss.at[8], rs.at[8], (sib, z)),
        ]

        def got(n, view):
            remote(view, view, ss.at[n], rs.at[n], (sib, z)).wait_recv()

        def start_own():
            for copy in own:
                copy.start()

        def forward_near():
            got(1, buf.at[xn])
            fwd[0].start()
            fwd[2].start()
            got(2, buf.at[yn])
            fwd[1].start()
            fwd[3].start()

        def forward_diagonal():
            got(3, buf.at[dg, lower])
            fwd[4].start()
            got(4, buf.at[dg, upper])
            fwd[5].start()

        def all_in():
            got(0, buf.at[sib])
            got(5, buf.at[sib_xn])
            got(6, buf.at[sib_yn])
            got(7, buf.at[sib_dg, lower])
            got(8, buf.at[sib_dg, upper])

        def all_sent():
            for copy in own + fwd:
                copy.wait_send()

        return start_own, forward_near, forward_diagonal, all_in, all_sent

    kv_moves = moves(kv, kv_send, kv_recv)
    kv_moves[0]()
    doc_copies = []
    for step in range(1, ctx):
        peer = lax.rem(c + step, ctx)
        doc_copies.append(
            remote(docs.at[c], docs.at[c], doc_send.at[step], doc_recv.at[step], (peer, z))
        )
        doc_copies[-1].start()
    kv_moves[1]()
    kv_moves[2]()
    for step in range(1, ctx):
        source = lax.rem(c + ctx - step, ctx)
        remote(
            docs.at[source], docs.at[source], doc_send.at[step], doc_recv.at[step], (source, z)
        ).wait_recv()
    kv_moves[3]()

    lane = lax.broadcasted_iota(jnp.int32, (tokens, HD), 1)

    def down(slot):
        across = docs[slot][0:1, :].astype(F32)
        return jnp.broadcast_to(across, (HD, tokens)).T.astype(jnp.int32)

    q_mask[...] = jnp.where(lane == down(c), 1.0, 0.0).astype(BF16)

    def mask_slot(slot, _):
        apart = (lane < DOCS) & (lane != down(slot))
        k_mask[slot] = jnp.where(apart, -(2.0**100), 0.0).astype(BF16)
        for g in range(kv_here):
            v = kv[slot, :, (kv_here + g) * HD : (kv_here + g + 1) * HD]
            v_down[slot, g] = v.astype(F32).T.astype(BF16)
        return 0

    lax.fori_loop(0, ctx, mask_slot, 0)

    pair = 2
    keys = pair * tokens
    blocks = c // pair

    def attend(p):
        t = chunk(p)
        begin = pl.multiple_of(t * rows, rows)
        q_extra = q_mask[pl.ds(begin, rows), :]
        qs = [
            jnp.concatenate(
                [
                    jnp.concatenate(
                        [
                            q_ref[
                                pl.ds(begin, rows),
                                (g * per_kv + h) * HD : (g * per_kv + h + 1) * HD,
                            ],
                            q_extra,
                        ],
                        axis=1,
                    )
                    for h in range(per_kv)
                ],
                axis=0,
            )
            for g in range(kv_here)
        ]

        def body(b, carry, bias=None):
            here = pl.ds(pair * b, pair)
            extra = k_mask[here].reshape(keys, HD)
            ones = jnp.ones((16, keys), BF16)
            state = []
            for g in range(kv_here):
                old_max, acc = carry[g]
                k = kv[here, :, g * HD : (g + 1) * HD].reshape(keys, HD)
                v = jnp.concatenate([v_down[pair * b + n, g] for n in range(pair)], axis=1)
                s = lax.dot_general(
                    jnp.concatenate([k, extra], axis=1), qs[g], (((1,), (1,)), ((), ())),
                    preferred_element_type=F32,
                ) * SCALE2
                if bias is not None:
                    s = s + bias
                new_max = jnp.maximum(old_max, jnp.max(s, axis=0, keepdims=True))
                weights = jnp.exp2(s - new_max).astype(BF16)
                acc = acc * jnp.exp2(old_max - new_max) + jnp.dot(
                    jnp.concatenate([v, ones], axis=0), weights, preferred_element_type=F32
                )
                state.append((new_max, acc))
            return tuple(state)

        lines = per_kv * rows
        state = lax.fori_loop(
            0,
            blocks,
            body,
            ((jnp.full((1, lines), -1e30, F32), jnp.zeros((HD + 16, lines), F32)),) * kv_here,
        )
        line = lax.broadcasted_iota(jnp.int32, (keys, lines), 1)
        q_pos = c * tokens + t * rows + lax.rem(line, rows)
        k_pos = blocks * keys + lax.broadcasted_iota(jnp.int32, (keys, lines), 0)
        state = body(blocks, state, jnp.where(k_pos <= q_pos, 0.0, -1e30).astype(F32))
        for g in range(kv_here):
            acc = state[g][1]
            o = (acc[:HD] / acc[HD : HD + 1]).T.astype(BF16)
            for h in range(per_kv):
                att[p, c, :, (g * per_kv + h) * HD : (g * per_kv + h + 1) * HD] = o[
                    h * rows : (h + 1) * rows
                ]

    def end_hop(p, j):
        return remote(
            part.at[p, j], zin.at[(0, 2, 3)[p], j], z_send.at[p, j],
            z_recv.at[(0, 2, 3)[p], j], (c, ahead),
        )

    def mid_hop(p, j):
        return remote(
            part.at[p, j], zin.at[(1, 0, 4)[p], j], z_send.at[p, j],
            z_recv.at[(1, 0, 4)[p], j], (c, (ahead, behind, ahead)[p]),
        )

    def z_got(slot, j):
        remote(
            zin.at[slot, j], zin.at[slot, j], z_send.at[0, j], z_recv.at[slot, j], (c, ahead)
        ).wait_recv()

    def project(p):
        def body(j, _):
            a = att[p].reshape(ctx * rows, att.shape[3])
            w = w_ref[:, pl.ds(pl.multiple_of(j * unit, unit), unit)]
            part[p, j] = jnp.dot(a, w, preferred_element_type=F32).astype(BF16)
            if p < 3:
                @pl.when(mid == 0)
                def _():
                    end_hop(p, j).start()

            return 0

        lax.fori_loop(0, UNITS, body, 0)

    def pass_on(*units):
        @pl.when(mid == 1)
        def _():
            for p, j in units:
                z_got(p, j)
                part[p, j] = (part[p, j].astype(F32) + zin[p, j].astype(F32)).astype(BF16)
                mid_hop(p, j).start()

    w_copy.wait()
    steps = [
        moves(att.at[p], att_send.at[p], att_recv.at[p]) for p in range(4)
    ]
    attend(0)
    steps[0][0]()
    attend(1)
    steps[0][1]()
    steps[1][0]()
    steps[0][2]()
    steps[0][3]()
    project(0)
    attend(2)
    steps[1][1]()
    steps[2][0]()
    steps[1][2]()
    steps[1][3]()
    project(1)
    pass_on((0, 0))
    attend(3)
    steps[2][1]()
    steps[3][0]()
    steps[2][2]()
    steps[2][3]()
    project(2)
    pass_on((0, 1), (0, 2))
    steps[3][1]()
    steps[3][2]()
    pass_on((1, 0))
    steps[3][3]()
    project(3)
    pass_on((0, 3), (1, 1), (2, 0), (1, 2), (2, 1), (1, 3), (2, 2), (2, 3))

    x_copies = []
    for j in range(UNITS):
        @pl.when(mid == 0)
        def _():
            z_got(0, j)
            total = part[3, j].astype(F32) + zin[0, j].astype(F32)
            fin[j] = total.astype(BF16).reshape(fin.shape[1:])

        @pl.when(mid == 1)
        def _():
            z_got(4, j)
            z_got(3, j)
            total = part[3, j].astype(F32) + zin[3, j].astype(F32) + zin[4, j].astype(F32)
            fin[j] = total.astype(BF16).reshape(fin.shape[1:])

        columns = pl.ds(pl.multiple_of(c * width + j * unit, unit), unit)
        for step in range(1, ctx):
            peer = lax.rem(c + step, ctx)
            x_copies.append(
                remote(
                    fin.at[j, peer], out_ref.at[:, columns], x_send.at[step, j],
                    x_recv.at[step, j], (peer, z),
                )
            )
            x_copies[-1].start()
        out_ref[:, columns] = fin[j, c]

    for j in range(UNITS):
        for step in range(1, ctx):
            source = lax.rem(c + ctx - step, ctx)
            columns = pl.ds(pl.multiple_of(source * width + j * unit, unit), unit)
            remote(
                fin.at[j, source], out_ref.at[:, columns], x_send.at[step, j],
                x_recv.at[step, j], (source, z),
            ).wait_recv()

    kv_moves[4]()
    for copy in doc_copies + x_copies:
        copy.wait_send()
    for step in steps:
        step[4]()

    @pl.when(mid == 0)
    def _():
        for p in range(3):
            for j in range(UNITS):
                end_hop(p, j).wait_send()

    @pl.when(mid == 1)
    def _():
        for p in range(3):
            for j in range(UNITS):
                mid_hop(p, j).wait_send()


def fused(ctx, tp, queries, key_rows, value_rows, documents, out_weight):
    tokens, heads_width = queries.shape
    kv_here = heads_width // HD // (HEADS // KV_HEADS)
    rows = tokens // tp
    depth, width = out_weight.shape
    unit = width // UNITS
    vmem = pl.BlockSpec(memory_space=pltpu.VMEM)
    dma = pltpu.SemaphoreType.DMA
    return pl.pallas_call(
        fused_kernel,
        out_shape=jax.ShapeDtypeStruct((rows, width * ctx), BF16),
        in_specs=[vmem] * 4 + [pl.BlockSpec(memory_space=pl.ANY)],
        out_specs=vmem,
        scratch_shapes=[
            pltpu.VMEM((depth, width), BF16),
            pltpu.VMEM((ctx, tokens, 2 * kv_here * HD), BF16),
            pltpu.VMEM((ctx, 8, tokens), jnp.int32),
            pltpu.VMEM((ctx, tokens, HD), BF16),
            pltpu.VMEM((tokens, HD), BF16),
            pltpu.VMEM((ctx, kv_here, HD, tokens), BF16),
            pltpu.VMEM((tp, ctx, rows, heads_width), BF16),
            pltpu.VMEM((tp, UNITS, ctx * rows, unit), BF16),
            pltpu.VMEM((5, UNITS, ctx * rows, unit), BF16),
            pltpu.VMEM((UNITS, ctx, rows, unit), BF16),
            dma,
            dma((9,)),
            dma((9,)),
            dma((ctx,)),
            dma((ctx,)),
            dma((tp, 9)),
            dma((tp, 9)),
            dma((3, UNITS)),
            dma((5, UNITS)),
            dma((ctx, UNITS)),
            dma((ctx, UNITS)),
        ],
        compiler_params=pltpu.CompilerParams(
            collective_id=0, has_side_effects=True, vmem_limit_bytes=56 * 1024 * 1024
        ),
    )(
        queries, key_rows, value_rows, documents.reshape(1, tokens), out_weight,
    )


def general(ctx, tp, queries, key_rows, value_rows, documents, out_weight):
    tokens = queries.shape[0]
    heads_here = queries.shape[1] // HD
    group_size = HEADS // KV_HEADS
    kv_here = max(1, heads_here // group_size)
    per_kv = heads_here // kv_here
    kv_first = lax.axis_index("tp") * heads_here // group_size
    own_keys = lax.dynamic_slice_in_dim(key_rows, kv_first * HD, kv_here * HD, 1)
    own_values = lax.dynamic_slice_in_dim(value_rows, kv_first * HD, kv_here * HD, 1)
    q = queries.reshape(tokens, kv_here, per_kv, HD)
    keys = lax.all_gather(own_keys, "ctx", axis=0, tiled=True).reshape(-1, kv_here, HD)
    values = lax.all_gather(own_values, "ctx", axis=0, tiled=True).reshape(-1, kv_here, HD)
    docs = lax.all_gather(documents, "ctx", axis=0, tiled=True)
    q_pos = lax.axis_index("ctx") * tokens + jnp.arange(tokens, dtype=jnp.int32)
    k_pos = jnp.arange(keys.shape[0], dtype=jnp.int32)
    allowed = (k_pos[None, :] <= q_pos[:, None]) & (docs[None, :] == documents[:, None])
    scores = jnp.einsum("tghd,ngd->ghtn", q, keys, preferred_element_type=F32) / math.sqrt(HD)
    row_max = jnp.max(jnp.where(allowed, scores, -1e30), axis=3, keepdims=True)
    weights = jnp.where(allowed, jnp.exp(scores - row_max), 0.0)
    total = jnp.transpose(jnp.sum(weights, axis=3), (2, 0, 1))[..., None]
    mixed = jnp.einsum("ghtn,ngd->tghd", weights.astype(BF16), values, preferred_element_type=F32)
    attended = (mixed / total).astype(BF16).reshape(tokens, heads_here * HD)
    gathered = lax.all_gather(attended, "ctx", axis=0, tiled=True)
    terms = jnp.dot(gathered, out_weight, preferred_element_type=F32).astype(BF16)
    terms = jnp.transpose(terms.reshape(ctx, tp, tokens // tp, -1), (1, 0, 2, 3))
    summed = lax.psum_scatter(terms, "tp", scatter_dimension=0, tiled=True)[0]
    return lax.all_to_all(summed, "ctx", split_axis=0, concat_axis=2, tiled=True)[0]


def solution(mesh):
    ctx, tp = mesh.shape["ctx"], mesh.shape["tp"]
    on_device = functools.partial(fused if (ctx, tp) == (8, 4) else general, ctx, tp)
    in_specs = (P("ctx", "tp"), P("ctx", None), P("ctx", None), P("ctx"), P("tp", "ctx"))
    return jax.shard_map(
        on_device, mesh=mesh, in_specs=in_specs,
        out_specs=P(("ctx", "tp"), None), check_vma=False,
    )
```

```python
import functools
import math

import jax
import jax.numpy as jnp
from jax import lax
from jax.experimental import pallas as pl
from jax.experimental.pallas import tpu as pltpu
from jax.sharding import PartitionSpec as P

HEADS = 64
KV_HEADS = 8
HD = 128
DOCS = 4
MESH = pl.DeviceIdType.MESH
F32 = jnp.float32
BF16 = jnp.bfloat16
SCALE2 = math.log2(math.e) / math.sqrt(HD)
UNITS = 4


def fused_kernel(
    q_ref, k_ref, v_ref, drow_ref, w_hbm, out_ref,
    w_ref, kv, docs, k_mask, q_mask, v_down, att, part, zin, fin,
    w_sem, kv_send, kv_recv, doc_send, doc_recv,
    att_send, att_recv, z_send, z_recv, x_send, x_recv,
):
    c = lax.axis_index("ctx")
    z = lax.axis_index("tp")
    ctx = kv.shape[0]
    tokens = q_ref.shape[0]
    rows = att.shape[2]
    kv_here = kv.shape[2] // (2 * HD)
    per_kv = q_ref.shape[1] // HD // kv_here
    unit = part.shape[3]
    width = UNITS * unit

    y, x, core = c // 4, (c // 2) % 2, c % 2

    def at(yy, xx, cc):
        return yy * 4 + xx * 2 + cc

    sib, xn, yn = at(y, x, 1 - core), at(y, 1 - x, core), at(1 - y, x, core)
    dg = at(1 - y, 1 - x, core)
    sib_xn, sib_yn = at(y, 1 - x, 1 - core), at(1 - y, x, 1 - core)
    sib_dg = at(1 - y, 1 - x, 1 - core)

    far = z // 2
    out = 1 - 2 * far
    mid = z * (1 - far) + (3 - z) * far
    ahead, behind = z + out, z - out

    def chunk(p):
        mirrored = (1 - mid) * (3 - p) + mid * (3, 0, 2, 1)[p]
        return mirrored * (1 - far) + (3 - mirrored) * far

    def remote(src, dst, ss, rs, device):
        return pltpu.make_async_remote_copy(
            src_ref=src, dst_ref=dst, send_sem=ss, recv_sem=rs,
            device_id=device, device_id_type=MESH,
        )

    w_copy = pltpu.make_async_copy(w_hbm, w_ref, w_sem)
    w_copy.start()

    barrier = pltpu.get_barrier_semaphore()
    for step in range(1, ctx):
        pl.semaphore_signal(
            barrier, inc=1, device_id=(lax.rem(c + step, ctx), z), device_id_type=MESH
        )
    pl.semaphore_signal(barrier, inc=1, device_id=(c, ahead), device_id_type=MESH)

    @pl.when(mid == 1)
    def _():
        pl.semaphore_signal(barrier, inc=1, device_id=(c, behind), device_id_type=MESH)

    first = pl.multiple_of(z * kv_here * HD, kv_here * HD)
    kv[c, :, : kv_here * HD] = k_ref[:, pl.ds(first, kv_here * HD)]
    kv[c, :, kv_here * HD :] = v_ref[:, pl.ds(first, kv_here * HD)]
    docs[c] = jnp.broadcast_to(drow_ref[...], docs.shape[1:])
    pl.semaphore_wait(barrier, ctx + mid)

    def moves(buf, ss, rs):
        half = buf.shape[1] // 2
        lower, upper = pl.ds(0, half), pl.ds(half, half)
        own = [
            remote(buf.at[c], buf.at[c], ss.at[0], rs.at[0], (sib, z)),
            remote(buf.at[c], buf.at[c], ss.at[1], rs.at[1], (xn, z)),
            remote(buf.at[c], buf.at[c], ss.at[2], rs.at[2], (yn, z)),
        ]
        fwd = [
            remote(buf.at[xn, lower], buf.at[xn, lower], ss.at[3], rs.at[3], (yn, z)),
            remote(buf.at[yn, upper], buf.at[yn, upper], ss.at[4], rs.at[4], (xn, z)),
            remote(buf.at[xn], buf.at[xn], ss.at[5], rs.at[5], (sib, z)),
            remote(buf.at[yn], buf.at[yn], ss.at[6], rs.at[6], (sib, z)),
            remote(buf.at[dg, lower], buf.at[dg, lower], ss.at[7], rs.at[7], (sib, z)),
            remote(buf.at[dg, upper], buf.at[dg, upper], ss.at[8], rs.at[8], (sib, z)),
        ]

        def got(n, view):
            remote(view, view, ss.at[n], rs.at[n], (sib, z)).wait_recv()

        def start_own():
            for copy in own:
                copy.start()

        def forward_near():
            got(1, buf.at[xn])
            fwd[0].start()
            fwd[2].start()
            got(2, buf.at[yn])
            fwd[1].start()
            fwd[3].start()

        def forward_diagonal():
            got(3, buf.at[dg, lower])
            fwd[4].start()
            got(4, buf.at[dg, upper])
            fwd[5].start()

        def all_in():
            got(0, buf.at[sib])
            got(5, buf.at[sib_xn])
            got(6, buf.at[sib_yn])
            got(7, buf.at[sib_dg, lower])
            got(8, buf.at[sib_dg, upper])

        def all_sent():
            for copy in own + fwd:
                copy.wait_send()

        return start_own, forward_near, forward_diagonal, all_in, all_sent

    kv_moves = moves(kv, kv_send, kv_recv)
    doc_copies = []
    for step in range(1, ctx):
        peer = lax.rem(c + step, ctx)
        doc_copies.append(
            remote(docs.at[c], docs.at[c], doc_send.at[step], doc_recv.at[step], (peer, z))
        )
        doc_copies[-1].start()
    kv_moves[0]()
    for step in range(1, ctx):
        source = lax.rem(c + ctx - step, ctx)
        remote(
            docs.at[source], docs.at[source], doc_send.at[step], doc_recv.at[step], (source, z)
        ).wait_recv()

    lane = lax.broadcasted_iota(jnp.int32, (tokens, HD), 1)

    def down(slot):
        across = docs[slot][0:1, :].astype(F32)
        return jnp.broadcast_to(across, (HD, tokens)).T.astype(jnp.int32)

    q_mask[...] = jnp.where(lane == down(c), 1.0, 0.0).astype(BF16)

    def mask_slot(slot, _):
        apart = (lane < DOCS) & (lane != down(slot))
        k_mask[slot] = jnp.where(apart, -(2.0**100), 0.0).astype(BF16)
        return 0

    lax.fori_loop(0, ctx, mask_slot, 0)

    def turn(*slots):
        for slot in slots:
            for g in range(kv_here):
                v = kv[slot, :, (kv_here + g) * HD : (kv_here + g + 1) * HD]
                v_down[slot, g] = v.astype(F32).T.astype(BF16)

    turn(c)
    kv_moves[1]()
    turn(xn, yn)
    kv_moves[2]()
    turn(dg)
    kv_moves[3]()
    turn(sib, sib_xn, sib_yn, sib_dg)

    pair = 2
    keys = pair * tokens
    blocks = c // pair

    def attend(p):
        t = chunk(p)
        begin = pl.multiple_of(t * rows, rows)
        q_extra = q_mask[pl.ds(begin, rows), :]
        qs = [
            jnp.concatenate(
                [
                    jnp.concatenate(
                        [
                            q_ref[
                                pl.ds(begin, rows),
                                (g * per_kv + h) * HD : (g * per_kv + h + 1) * HD,
                            ],
                            q_extra,
                        ],
                        axis=1,
                    )
                    for h in range(per_kv)
                ],
                axis=0,
            )
            for g in range(kv_here)
        ]

        def body(b, carry, bias=None):
            here = pl.ds(pair * b, pair)
            extra = k_mask[here].reshape(keys, HD)
            ones = jnp.ones((16, keys), BF16)
            state = []
            for g in range(kv_here):
                old_max, acc = carry[g]
                k = kv[here, :, g * HD : (g + 1) * HD].reshape(keys, HD)
                v = jnp.concatenate([v_down[pair * b + n, g] for n in range(pair)], axis=1)
                s = lax.dot_general(
                    jnp.concatenate([k, extra], axis=1), qs[g], (((1,), (1,)), ((), ())),
                    preferred_element_type=F32,
                ) * SCALE2
                if bias is not None:
                    s = s + bias
                new_max = jnp.maximum(old_max, jnp.max(s, axis=0, keepdims=True))
                weights = jnp.exp2(s - new_max).astype(BF16)
                acc = acc * jnp.exp2(old_max - new_max) + jnp.dot(
                    jnp.concatenate([v, ones], axis=0), weights, preferred_element_type=F32
                )
                state.append((new_max, acc))
            return tuple(state)

        lines = per_kv * rows
        state = lax.fori_loop(
            0,
            blocks,
            body,
            ((jnp.full((1, lines), -1e30, F32), jnp.zeros((HD + 16, lines), F32)),) * kv_here,
        )
        line = lax.broadcasted_iota(jnp.int32, (keys, lines), 1)
        q_pos = c * tokens + t * rows + lax.rem(line, rows)
        k_pos = blocks * keys + lax.broadcasted_iota(jnp.int32, (keys, lines), 0)
        state = body(blocks, state, jnp.where(k_pos <= q_pos, 0.0, -1e30).astype(F32))
        for g in range(kv_here):
            acc = state[g][1]
            o = (acc[:HD] / acc[HD : HD + 1]).T.astype(BF16)
            for h in range(per_kv):
                att[p, c, :, (g * per_kv + h) * HD : (g * per_kv + h + 1) * HD] = o[
                    h * rows : (h + 1) * rows
                ]

    def end_hop(p, j):
        return remote(
            part.at[p, j], zin.at[(0, 2, 3)[p], j], z_send.at[p, j],
            z_recv.at[(0, 2, 3)[p], j], (c, ahead),
        )

    def mid_hop(p, j):
        return remote(
            part.at[p, j], zin.at[(1, 0, 4)[p], j], z_send.at[p, j],
            z_recv.at[(1, 0, 4)[p], j], (c, (ahead, behind, ahead)[p]),
        )

    def z_got(slot, j):
        remote(
            zin.at[slot, j], zin.at[slot, j], z_send.at[0, j], z_recv.at[slot, j], (c, ahead)
        ).wait_recv()

    def project(p):
        def body(j, _):
            a = att[p].reshape(ctx * rows, att.shape[3])
            w = w_ref[:, pl.ds(pl.multiple_of(j * unit, unit), unit)]
            part[p, j] = jnp.dot(a, w, preferred_element_type=F32).astype(BF16)
            if p < 3:
                @pl.when(mid == 0)
                def _():
                    end_hop(p, j).start()

            return 0

        lax.fori_loop(0, UNITS, body, 0)

    def pass_on(*units):
        @pl.when(mid == 1)
        def _():
            for p, j in units:
                z_got(p, j)
                part[p, j] = (part[p, j].astype(F32) + zin[p, j].astype(F32)).astype(BF16)
                mid_hop(p, j).start()

    w_copy.wait()
    steps = [
        moves(att.at[p], att_send.at[p], att_recv.at[p]) for p in range(4)
    ]
    attend(0)
    steps[0][0]()
    attend(1)
    steps[0][1]()
    steps[1][0]()
    steps[0][2]()
    steps[0][3]()
    project(0)
    attend(2)
    steps[1][1]()
    steps[2][0]()
    steps[1][2]()
    steps[1][3]()
    project(1)
    pass_on((0, 0))
    attend(3)
    steps[2][1]()
    steps[3][0]()
    steps[2][2]()
    steps[2][3]()
    project(2)
    pass_on((0, 1), (0, 2))
    steps[3][1]()
    steps[3][2]()
    pass_on((1, 0))
    steps[3][3]()
    project(3)
    pass_on((0, 3), (1, 1), (2, 0), (1, 2), (2, 1), (1, 3), (2, 2), (2, 3))

    x_copies = []
    for j in range(UNITS):
        @pl.when(mid == 0)
        def _():
            z_got(0, j)
            total = part[3, j].astype(F32) + zin[0, j].astype(F32)
            fin[j] = total.astype(BF16).reshape(fin.shape[1:])

        @pl.when(mid == 1)
        def _():
            z_got(4, j)
            z_got(3, j)
            total = part[3, j].astype(F32) + zin[3, j].astype(F32) + zin[4, j].astype(F32)
            fin[j] = total.astype(BF16).reshape(fin.shape[1:])

        columns = pl.ds(pl.multiple_of(c * width + j * unit, unit), unit)
        for step in range(1, ctx):
            peer = lax.rem(c + step, ctx)
            x_copies.append(
                remote(
                    fin.at[j, peer], out_ref.at[:, columns], x_send.at[step, j],
                    x_recv.at[step, j], (peer, z),
                )
            )
            x_copies[-1].start()
        out_ref[:, columns] = fin[j, c]

    for j in range(UNITS):
        for step in range(1, ctx):
            source = lax.rem(c + ctx - step, ctx)
            columns = pl.ds(pl.multiple_of(source * width + j * unit, unit), unit)
            remote(
                fin.at[j, source], out_ref.at[:, columns], x_send.at[step, j],
                x_recv.at[step, j], (source, z),
            ).wait_recv()

    kv_moves[4]()
    for copy in doc_copies + x_copies:
        copy.wait_send()
    for step in steps:
        step[4]()

    @pl.when(mid == 0)
    def _():
        for p in range(3):
            for j in range(UNITS):
                end_hop(p, j).wait_send()

    @pl.when(mid == 1)
    def _():
        for p in range(3):
            for j in range(UNITS):
                mid_hop(p, j).wait_send()


def fused(ctx, tp, queries, key_rows, value_rows, documents, out_weight):
    tokens, heads_width = queries.shape
    kv_here = heads_width // HD // (HEADS // KV_HEADS)
    rows = tokens // tp
    depth, width = out_weight.shape
    unit = width // UNITS
    vmem = pl.BlockSpec(memory_space=pltpu.VMEM)
    dma = pltpu.SemaphoreType.DMA
    return pl.pallas_call(
        fused_kernel,
        out_shape=jax.ShapeDtypeStruct((rows, width * ctx), BF16),
        in_specs=[vmem] * 4 + [pl.BlockSpec(memory_space=pl.ANY)],
        out_specs=vmem,
        scratch_shapes=[
            pltpu.VMEM((depth, width), BF16),
            pltpu.VMEM((ctx, tokens, 2 * kv_here * HD), BF16),
            pltpu.VMEM((ctx, 8, tokens), jnp.int32),
            pltpu.VMEM((ctx, tokens, HD), BF16),
            pltpu.VMEM((tokens, HD), BF16),
            pltpu.VMEM((ctx, kv_here, HD, tokens), BF16),
            pltpu.VMEM((tp, ctx, rows, heads_width), BF16),
            pltpu.VMEM((tp, UNITS, ctx * rows, unit), BF16),
            pltpu.VMEM((5, UNITS, ctx * rows, unit), BF16),
            pltpu.VMEM((UNITS, ctx, rows, unit), BF16),
            dma,
            dma((9,)),
            dma((9,)),
            dma((ctx,)),
            dma((ctx,)),
            dma((tp, 9)),
            dma((tp, 9)),
            dma((3, UNITS)),
            dma((5, UNITS)),
            dma((ctx, UNITS)),
            dma((ctx, UNITS)),
        ],
        compiler_params=pltpu.CompilerParams(
            collective_id=0, has_side_effects=True, vmem_limit_bytes=56 * 1024 * 1024
        ),
    )(
        queries, key_rows, value_rows, documents.reshape(1, tokens), out_weight,
    )


def general(ctx, tp, queries, key_rows, value_rows, documents, out_weight):
    tokens = queries.shape[0]
    heads_here = queries.shape[1] // HD
    group_size = HEADS // KV_HEADS
    kv_here = max(1, heads_here // group_size)
    per_kv = heads_here // kv_here
    kv_first = lax.axis_index("tp") * heads_here // group_size
    own_keys = lax.dynamic_slice_in_dim(key_rows, kv_first * HD, kv_here * HD, 1)
    own_values = lax.dynamic_slice_in_dim(value_rows, kv_first * HD, kv_here * HD, 1)
    q = queries.reshape(tokens, kv_here, per_kv, HD)
    keys = lax.all_gather(own_keys, "ctx", axis=0, tiled=True).reshape(-1, kv_here, HD)
    values = lax.all_gather(own_values, "ctx", axis=0, tiled=True).reshape(-1, kv_here, HD)
    docs = lax.all_gather(documents, "ctx", axis=0, tiled=True)
    q_pos = lax.axis_index("ctx") * tokens + jnp.arange(tokens, dtype=jnp.int32)
    k_pos = jnp.arange(keys.shape[0], dtype=jnp.int32)
    allowed = (k_pos[None, :] <= q_pos[:, None]) & (docs[None, :] == documents[:, None])
    scores = jnp.einsum("tghd,ngd->ghtn", q, keys, preferred_element_type=F32) / math.sqrt(HD)
    row_max = jnp.max(jnp.where(allowed, scores, -1e30), axis=3, keepdims=True)
    weights = jnp.where(allowed, jnp.exp(scores - row_max), 0.0)
    total = jnp.transpose(jnp.sum(weights, axis=3), (2, 0, 1))[..., None]
    mixed = jnp.einsum("ghtn,ngd->tghd", weights.astype(BF16), values, preferred_element_type=F32)
    attended = (mixed / total).astype(BF16).reshape(tokens, heads_here * HD)
    gathered = lax.all_gather(attended, "ctx", axis=0, tiled=True)
    terms = jnp.dot(gathered, out_weight, preferred_element_type=F32).astype(BF16)
    terms = jnp.transpose(terms.reshape(ctx, tp, tokens // tp, -1), (1, 0, 2, 3))
    summed = lax.psum_scatter(terms, "tp", scatter_dimension=0, tiled=True)[0]
    return lax.all_to_all(summed, "ctx", split_axis=0, concat_axis=2, tiled=True)[0]


def solution(mesh):
    ctx, tp = mesh.shape["ctx"], mesh.shape["tp"]
    on_device = functools.partial(fused if (ctx, tp) == (8, 4) else general, ctx, tp)
    in_specs = (P("ctx", "tp"), P("ctx", None), P("ctx", None), P("ctx"), P("tp", "ctx"))
    return jax.shard_map(
        on_device, mesh=mesh, in_specs=in_specs,
        out_specs=P(("ctx", "tp"), None), check_vma=False,
    )
```

```python
import functools
import math

import jax
import jax.numpy as jnp
from jax import lax
from jax.experimental import pallas as pl
from jax.experimental.pallas import tpu as pltpu
from jax.sharding import PartitionSpec as P

HEADS = 64
KV_HEADS = 8
HD = 128
DOCS = 4
MESH = pl.DeviceIdType.MESH
F32 = jnp.float32
BF16 = jnp.bfloat16
SCALE2 = math.log2(math.e) / math.sqrt(HD)
UNITS = 4


def fused_kernel(
    q_ref, k_ref, v_ref, drow_ref, w_hbm, out_ref,
    w_ref, kv, docs, k_mask, q_mask, v_down, att, part, zin, fin,
    w_sem, kv_send, kv_recv, doc_send, doc_recv,
    att_send, att_recv, z_send, z_recv, x_send, x_recv,
):
    c = lax.axis_index("ctx")
    z = lax.axis_index("tp")
    ctx = kv.shape[0]
    tokens = q_ref.shape[0]
    rows = att.shape[2]
    kv_here = kv.shape[2] // (2 * HD)
    per_kv = q_ref.shape[1] // HD // kv_here
    unit = part.shape[3]
    width = UNITS * unit

    y, x, core = c // 4, (c // 2) % 2, c % 2

    def at(yy, xx, cc):
        return yy * 4 + xx * 2 + cc

    sib, xn, yn = at(y, x, 1 - core), at(y, 1 - x, core), at(1 - y, x, core)
    dg = at(1 - y, 1 - x, core)
    sib_xn, sib_yn = at(y, 1 - x, 1 - core), at(1 - y, x, 1 - core)
    sib_dg = at(1 - y, 1 - x, 1 - core)

    far = z // 2
    out = 1 - 2 * far
    mid = z * (1 - far) + (3 - z) * far
    ahead, behind = z + out, z - out

    def chunk(p):
        mirrored = (1 - mid) * (3 - p) + mid * (3, 0, 2, 1)[p]
        return mirrored * (1 - far) + (3 - mirrored) * far

    def remote(src, dst, ss, rs, device):
        return pltpu.make_async_remote_copy(
            src_ref=src, dst_ref=dst, send_sem=ss, recv_sem=rs,
            device_id=device, device_id_type=MESH,
        )

    w_copy = pltpu.make_async_copy(w_hbm, w_ref, w_sem)
    w_copy.start()

    barrier = pltpu.get_barrier_semaphore()
    for step in range(1, ctx):
        pl.semaphore_signal(
            barrier, inc=1, device_id=(lax.rem(c + step, ctx), z), device_id_type=MESH
        )
    pl.semaphore_signal(barrier, inc=1, device_id=(c, ahead), device_id_type=MESH)

    @pl.when(mid == 1)
    def _():
        pl.semaphore_signal(barrier, inc=1, device_id=(c, behind), device_id_type=MESH)

    first = pl.multiple_of(z * kv_here * HD, kv_here * HD)
    kv[c, :, : kv_here * HD] = k_ref[:, pl.ds(first, kv_here * HD)]
    kv[c, :, kv_here * HD :] = v_ref[:, pl.ds(first, kv_here * HD)]
    docs[c] = jnp.broadcast_to(drow_ref[...], docs.shape[1:])
    pl.semaphore_wait(barrier, ctx + mid)

    def moves(buf, ss, rs):
        half = buf.shape[1] // 2
        lower, upper = pl.ds(0, half), pl.ds(half, half)
        own = [
            remote(buf.at[c], buf.at[c], ss.at[0], rs.at[0], (sib, z)),
            remote(buf.at[c], buf.at[c], ss.at[1], rs.at[1], (xn, z)),
            remote(buf.at[c], buf.at[c], ss.at[2], rs.at[2], (yn, z)),
        ]
        fwd = [
            remote(buf.at[xn, lower], buf.at[xn, lower], ss.at[3], rs.at[3], (yn, z)),
            remote(buf.at[yn, upper], buf.at[yn, upper], ss.at[4], rs.at[4], (xn, z)),
            remote(buf.at[xn], buf.at[xn], ss.at[5], rs.at[5], (sib, z)),
            remote(buf.at[yn], buf.at[yn], ss.at[6], rs.at[6], (sib, z)),
            remote(buf.at[dg, lower], buf.at[dg, lower], ss.at[7], rs.at[7], (sib, z)),
            remote(buf.at[dg, upper], buf.at[dg, upper], ss.at[8], rs.at[8], (sib, z)),
        ]

        def got(n, view):
            remote(view, view, ss.at[n], rs.at[n], (sib, z)).wait_recv()

        def start_own():
            for copy in own:
                copy.start()

        def forward_near():
            got(1, buf.at[xn])
            fwd[0].start()
            fwd[2].start()
            got(2, buf.at[yn])
            fwd[1].start()
            fwd[3].start()

        def forward_diagonal():
            got(3, buf.at[dg, lower])
            fwd[4].start()
            got(4, buf.at[dg, upper])
            fwd[5].start()

        def all_in():
            got(0, buf.at[sib])
            got(5, buf.at[sib_xn])
            got(6, buf.at[sib_yn])
            got(7, buf.at[sib_dg, lower])
            got(8, buf.at[sib_dg, upper])

        def all_sent():
            for copy in own + fwd:
                copy.wait_send()

        return start_own, forward_near, forward_diagonal, all_in, all_sent

    kv_moves = moves(kv, kv_send, kv_recv)
    kv_moves[0]()
    doc_copies = []
    for step in range(1, ctx):
        peer = lax.rem(c + step, ctx)
        doc_copies.append(
            remote(docs.at[c], docs.at[c], doc_send.at[step], doc_recv.at[step], (peer, z))
        )
        doc_copies[-1].start()
    kv_moves[1]()
    kv_moves[2]()
    for step in range(1, ctx):
        source = lax.rem(c + ctx - step, ctx)
        remote(
            docs.at[source], docs.at[source], doc_send.at[step], doc_recv.at[step], (source, z)
        ).wait_recv()
    kv_moves[3]()

    lane = lax.broadcasted_iota(jnp.int32, (tokens, HD), 1)

    def down(slot):
        across = docs[slot][0:1, :].astype(F32)
        return jnp.broadcast_to(across, (HD, tokens)).T.astype(jnp.int32)

    q_mask[...] = jnp.where(lane == down(c), 1.0, 0.0).astype(BF16)

    def mask_slot(slot, _):
        apart = (lane < DOCS) & (lane != down(slot))
        k_mask[slot] = jnp.where(apart, -(2.0**100), 0.0).astype(BF16)
        for g in range(kv_here):
            v = kv[slot, :, (kv_here + g) * HD : (kv_here + g + 1) * HD]
            v_down[slot, g] = v.astype(F32).T.astype(BF16)
        return 0

    lax.fori_loop(0, ctx, mask_slot, 0)

    pair = 2
    keys = pair * tokens
    blocks = c // pair

    def attend(p):
        t = chunk(p)
        begin = pl.multiple_of(t * rows, rows)
        q_extra = q_mask[pl.ds(begin, rows), :]
        qs = [
            jnp.concatenate(
                [
                    jnp.concatenate(
                        [
                            q_ref[
                                pl.ds(begin, rows),
                                (g * per_kv + h) * HD : (g * per_kv + h + 1) * HD,
                            ],
                            q_extra,
                        ],
                        axis=1,
                    )
                    for h in range(per_kv)
                ],
                axis=0,
            )
            for g in range(kv_here)
        ]

        def body(b, carry, bias=None):
            here = pl.ds(pair * b, pair)
            extra = k_mask[here].reshape(keys, HD)
            ones = jnp.ones((16, keys), BF16)
            state = []
            for g in range(kv_here):
                old_max, acc = carry[g]
                k = kv[here, :, g * HD : (g + 1) * HD].reshape(keys, HD)
                v = jnp.concatenate([v_down[pair * b + n, g] for n in range(pair)], axis=1)
                s = lax.dot_general(
                    jnp.concatenate([k, extra], axis=1), qs[g], (((1,), (1,)), ((), ())),
                    preferred_element_type=F32,
                ) * SCALE2
                if bias is not None:
                    s = s + bias
                new_max = jnp.maximum(old_max, jnp.max(s, axis=0, keepdims=True))
                weights = jnp.exp2(s - new_max).astype(BF16)
                acc = acc * jnp.exp2(old_max - new_max) + jnp.dot(
                    jnp.concatenate([v, ones], axis=0), weights, preferred_element_type=F32
                )
                state.append((new_max, acc))
            return tuple(state)

        lines = per_kv * rows
        state = lax.fori_loop(
            0,
            blocks,
            body,
            ((jnp.full((1, lines), -1e30, F32), jnp.zeros((HD + 16, lines), F32)),) * kv_here,
        )
        line = lax.broadcasted_iota(jnp.int32, (keys, lines), 1)
        q_pos = c * tokens + t * rows + lax.rem(line, rows)
        k_pos = blocks * keys + lax.broadcasted_iota(jnp.int32, (keys, lines), 0)
        state = body(blocks, state, jnp.where(k_pos <= q_pos, 0.0, -1e30).astype(F32))
        for g in range(kv_here):
            acc = state[g][1]
            o = (acc[:HD] / acc[HD : HD + 1]).T.astype(BF16)
            for h in range(per_kv):
                att[p, c, :, (g * per_kv + h) * HD : (g * per_kv + h + 1) * HD] = o[
                    h * rows : (h + 1) * rows
                ]

    def end_hop(p, j):
        return remote(
            part.at[p, j], zin.at[(0, 2, 3)[p], j], z_send.at[p, j],
            z_recv.at[(0, 2, 3)[p], j], (c, ahead),
        )

    def mid_hop(p, j):
        return remote(
            part.at[p, j], zin.at[(1, 0, 4)[p], j], z_send.at[p, j],
            z_recv.at[(1, 0, 4)[p], j], (c, (ahead, behind, ahead)[p]),
        )

    def z_got(slot, j):
        remote(
            zin.at[slot, j], zin.at[slot, j], z_send.at[0, j], z_recv.at[slot, j], (c, ahead)
        ).wait_recv()

    def project(p):
        def body(j, _):
            a = att[p].reshape(ctx * rows, att.shape[3])
            w = w_ref[:, pl.ds(pl.multiple_of(j * unit, unit), unit)]
            part[p, j] = jnp.dot(a, w, preferred_element_type=F32).astype(BF16)
            if p < 3:
                @pl.when(mid == 0)
                def _():
                    end_hop(p, j).start()

            return 0

        lax.fori_loop(0, UNITS, body, 0)

    def pass_on(*units):
        @pl.when(mid == 1)
        def _():
            for p, j in units:
                z_got(p, j)
                part[p, j] = (part[p, j].astype(F32) + zin[p, j].astype(F32)).astype(BF16)
                mid_hop(p, j).start()

    w_copy.wait()
    steps = [
        moves(att.at[p], att_send.at[p], att_recv.at[p]) for p in range(4)
    ]
    attend(0)
    steps[0][0]()
    steps[0][1]()
    steps[0][2]()
    steps[0][3]()
    project(0)
    attend(1)
    steps[1][0]()
    attend(2)
    steps[1][1]()
    steps[2][0]()
    steps[1][2]()
    steps[1][3]()
    project(1)
    pass_on((0, 0))
    attend(3)
    steps[2][1]()
    steps[3][0]()
    steps[2][2]()
    steps[2][3]()
    project(2)
    pass_on((0, 1), (0, 2))
    steps[3][1]()
    steps[3][2]()
    pass_on((1, 0))
    steps[3][3]()
    project(3)
    pass_on((0, 3), (1, 1), (2, 0), (1, 2), (2, 1), (1, 3), (2, 2), (2, 3))

    x_copies = []
    for j in range(UNITS):
        @pl.when(mid == 0)
        def _():
            z_got(0, j)
            total = part[3, j].astype(F32) + zin[0, j].astype(F32)
            fin[j] = total.astype(BF16).reshape(fin.shape[1:])

        @pl.when(mid == 1)
        def _():
            z_got(4, j)
            z_got(3, j)
            total = part[3, j].astype(F32) + zin[3, j].astype(F32) + zin[4, j].astype(F32)
            fin[j] = total.astype(BF16).reshape(fin.shape[1:])

        columns = pl.ds(pl.multiple_of(c * width + j * unit, unit), unit)
        for step in range(1, ctx):
            peer = lax.rem(c + step, ctx)
            x_copies.append(
                remote(
                    fin.at[j, peer], out_ref.at[:, columns], x_send.at[step, j],
                    x_recv.at[step, j], (peer, z),
                )
            )
            x_copies[-1].start()
        out_ref[:, columns] = fin[j, c]

    for j in range(UNITS):
        for step in range(1, ctx):
            source = lax.rem(c + ctx - step, ctx)
            columns = pl.ds(pl.multiple_of(source * width + j * unit, unit), unit)
            remote(
                fin.at[j, source], out_ref.at[:, columns], x_send.at[step, j],
                x_recv.at[step, j], (source, z),
            ).wait_recv()

    kv_moves[4]()
    for copy in doc_copies + x_copies:
        copy.wait_send()
    for step in steps:
        step[4]()

    @pl.when(mid == 0)
    def _():
        for p in range(3):
            for j in range(UNITS):
                end_hop(p, j).wait_send()

    @pl.when(mid == 1)
    def _():
        for p in range(3):
            for j in range(UNITS):
                mid_hop(p, j).wait_send()


def fused(ctx, tp, queries, key_rows, value_rows, documents, out_weight):
    tokens, heads_width = queries.shape
    kv_here = heads_width // HD // (HEADS // KV_HEADS)
    rows = tokens // tp
    depth, width = out_weight.shape
    unit = width // UNITS
    vmem = pl.BlockSpec(memory_space=pltpu.VMEM)
    dma = pltpu.SemaphoreType.DMA
    return pl.pallas_call(
        fused_kernel,
        out_shape=jax.ShapeDtypeStruct((rows, width * ctx), BF16),
        in_specs=[vmem] * 4 + [pl.BlockSpec(memory_space=pl.ANY)],
        out_specs=vmem,
        scratch_shapes=[
            pltpu.VMEM((depth, width), BF16),
            pltpu.VMEM((ctx, tokens, 2 * kv_here * HD), BF16),
            pltpu.VMEM((ctx, 8, tokens), jnp.int32),
            pltpu.VMEM((ctx, tokens, HD), BF16),
            pltpu.VMEM((tokens, HD), BF16),
            pltpu.VMEM((ctx, kv_here, HD, tokens), BF16),
            pltpu.VMEM((tp, ctx, rows, heads_width), BF16),
            pltpu.VMEM((tp, UNITS, ctx * rows, unit), BF16),
            pltpu.VMEM((5, UNITS, ctx * rows, unit), BF16),
            pltpu.VMEM((UNITS, ctx, rows, unit), BF16),
            dma,
            dma((9,)),
            dma((9,)),
            dma((ctx,)),
            dma((ctx,)),
            dma((tp, 9)),
            dma((tp, 9)),
            dma((3, UNITS)),
            dma((5, UNITS)),
            dma((ctx, UNITS)),
            dma((ctx, UNITS)),
        ],
        compiler_params=pltpu.CompilerParams(
            collective_id=0, has_side_effects=True, vmem_limit_bytes=56 * 1024 * 1024
        ),
    )(
        queries, key_rows, value_rows, documents.reshape(1, tokens), out_weight,
    )


def general(ctx, tp, queries, key_rows, value_rows, documents, out_weight):
    tokens = queries.shape[0]
    heads_here = queries.shape[1] // HD
    group_size = HEADS // KV_HEADS
    kv_here = max(1, heads_here // group_size)
    per_kv = heads_here // kv_here
    kv_first = lax.axis_index("tp") * heads_here // group_size
    own_keys = lax.dynamic_slice_in_dim(key_rows, kv_first * HD, kv_here * HD, 1)
    own_values = lax.dynamic_slice_in_dim(value_rows, kv_first * HD, kv_here * HD, 1)
    q = queries.reshape(tokens, kv_here, per_kv, HD)
    keys = lax.all_gather(own_keys, "ctx", axis=0, tiled=True).reshape(-1, kv_here, HD)
    values = lax.all_gather(own_values, "ctx", axis=0, tiled=True).reshape(-1, kv_here, HD)
    docs = lax.all_gather(documents, "ctx", axis=0, tiled=True)
    q_pos = lax.axis_index("ctx") * tokens + jnp.arange(tokens, dtype=jnp.int32)
    k_pos = jnp.arange(keys.shape[0], dtype=jnp.int32)
    allowed = (k_pos[None, :] <= q_pos[:, None]) & (docs[None, :] == documents[:, None])
    scores = jnp.einsum("tghd,ngd->ghtn", q, keys, preferred_element_type=F32) / math.sqrt(HD)
    row_max = jnp.max(jnp.where(allowed, scores, -1e30), axis=3, keepdims=True)
    weights = jnp.where(allowed, jnp.exp(scores - row_max), 0.0)
    total = jnp.transpose(jnp.sum(weights, axis=3), (2, 0, 1))[..., None]
    mixed = jnp.einsum("ghtn,ngd->tghd", weights.astype(BF16), values, preferred_element_type=F32)
    attended = (mixed / total).astype(BF16).reshape(tokens, heads_here * HD)
    gathered = lax.all_gather(attended, "ctx", axis=0, tiled=True)
    terms = jnp.dot(gathered, out_weight, preferred_element_type=F32).astype(BF16)
    terms = jnp.transpose(terms.reshape(ctx, tp, tokens // tp, -1), (1, 0, 2, 3))
    summed = lax.psum_scatter(terms, "tp", scatter_dimension=0, tiled=True)[0]
    return lax.all_to_all(summed, "ctx", split_axis=0, concat_axis=2, tiled=True)[0]


def solution(mesh):
    ctx, tp = mesh.shape["ctx"], mesh.shape["tp"]
    on_device = functools.partial(fused if (ctx, tp) == (8, 4) else general, ctx, tp)
    in_specs = (P("ctx", "tp"), P("ctx", None), P("ctx", None), P("ctx"), P("tp", "ctx"))
    return jax.shard_map(
        on_device, mesh=mesh, in_specs=in_specs,
        out_specs=P(("ctx", "tp"), None), check_vma=False,
    )
```
